32 devices in a mesh: section: 2 (over core), expert: 4 (over z), tensor: 4 (over y, x).
Axes of the slice: x: 2, y: 2, z: 4, core: 2. Of those that a mesh axis runs over, the one named last changes fastest.
Arguments:
- inputs: bfloat16 [2, 512, 768], P(None, 'expert'), may hold values from -6 to 6
- cotangent: bfloat16 [2, 512, 768], P(None, 'expert'), may hold values from -6 to 6
- attn_gain: bfloat16 [2, 768], P('section', 'expert'), may hold values from 0.5 to 1.5
- query_weight: bfloat16 [2, 768, 768], P('section', 'expert', 'tensor'), may hold values from -0.21875 to 0.21875
- key_weight: bfloat16 [2, 768, 768], P('section', 'expert', 'tensor'), may hold values from -0.21875 to 0.21875
- value_weight: bfloat16 [2, 768, 768], P('section', 'expert', 'tensor'), may hold values from -0.21875 to 0.21875
- out_weight: bfloat16 [2, 768, 768], P('section', 'expert', 'tensor'), may hold values from -1.75 to 1.75
- rel_table: bfloat16 [2, 32, 12], P('section', 'expert', 'tensor'), may hold values from -4 to 4
- ffn_gain: bfloat16 [2, 768], P('section', 'expert'), may hold values from 0.5 to 1.5
- router_weight: bfloat16 [2, 768, 4], P('section', 'expert'), may hold values from -0.15625 to 0.15625
- expert_in: bfloat16 [2, 4, 768, 3072], P('section', 'expert', None, 'tensor'), may hold values from -0.21875 to 0.21875
- expert_out: bfloat16 [2, 4, 3072, 768], P('section', 'expert', 'tensor'), may hold values from -0.625 to 0.625
- routes: int32 [2, 2, 512, 1], P('section', None, 'expert'), may hold values from 0 to 3; in each aligned block of 128 rows (0 to 127, 128 to 255, ..., all dimensions but the last counted through in order) at most 40 rows name the same one
- segments: int32 [2, 512], P(None, 'expert'), may hold values from 0 to 15, never falling along the last dimension, each value on 1 to 64 neighbouring positions
Outputs:
- section_outputs: bfloat16 [2, 2, 512, 768], P('section', None, 'expert')
- input_grads: bfloat16 [2, 2, 512, 768], P('section', None, 'expert')
- grad_attn_gain: float32 [2, 768], P('section', 'expert')
- grad_query_weight: float32 [2, 768, 768], P('section', 'expert', 'tensor')
- grad_key_weight: float32 [2, 768, 768], P('section', 'expert', 'tensor')
- grad_value_weight: float32 [2, 768, 768], P('section', 'expert', 'tensor')
- grad_out_weight: float32 [2, 768, 768], P('section', 'expert', 'tensor')
- grad_rel_table: float32 [2, 32, 12], P('section', 'expert', 'tensor')
- grad_ffn_gain: float32 [2, 768], P('section', 'expert')
- grad_router_weight: float32 [2, 768, 4], P('section', 'expert')
- grad_expert_in: float32 [2, 4, 768, 3072], P('section', 'expert', None, 'tensor')
- grad_expert_out: float32 [2, 4, 3072, 768], P('section', 'expert', 'tensor')
The draws below stay inside these ranges and needn't reach their ends.
Inputs may be any that keep to these rules, and one draw needn't show every extreme that they name: `routes`: in each aligned block of 128 rows (one sequence of one micro-batch and layer) no expert is named by more than 40 rows, a bound that some block reaches. `segments`: document numbers never fall along the tokens; a document holds at most 64 tokens, and one holds exactly that many.
All inputs are finite; a program needn't handle non-finite values.
Results may differ from the reference program's by a relative error of at most 0.035.
Values may be sent and summed in bfloat16 or wider, within the bound.
A program may use at most 128 MiB of HBM per device.

```python
import math
import jax
import jax.numpy as jnp
import numpy as np
from jax import lax

D = 768
HEADS = 12
HEAD_DIM = 64
FF = 3072
BUCKETS = 32
SEQ = 128
MICRO = 2
SECTIONS = 2
EXPERTS = 4
TOKENS = 512
CAP = 40
N_SECTION = 2
N_EXPERT = 4


def steps_of(key, shape, cuts, least, top_value):
    def one(dim, blocks):
        steps = jax.random.uniform(jax.random.fold_in(jax.random.fold_in(key, 6), dim), (blocks,), jnp.float32, least / len(cuts), top_value / len(cuts))
        return jnp.repeat(jnp.exp(steps), shape[dim] // blocks).reshape((-1,) + (1,) * (len(shape) - dim - 1))

    gain = one(*cuts[0])
    for cut in cuts[1:]:
        gain = gain * one(*cut)
    return gain


def length_profile(amount, total, limit, skew):
    weights = [(1 << 20) // math.isqrt(standing ** skew) + 1 for standing in range(2, amount + 1)]
    rest, holding = total - limit - (amount - 1), [1] * (amount - 1)
    while rest > 0:
        candidates = [i for i in range(amount - 1) if holding[i] < limit]
        mass, left = sum([weights[i] for i in candidates]), rest
        for i in candidates:
            addition = min(limit - holding[i], max(1, left * weights[i] // mass), rest)
            holding[i] = holding[i] + addition
            rest = rest - addition
    return np.array([limit] + holding)


def ragged_sizes(own_key, number_of, total, bound, slope):
    if number_of == 2:
        one = jax.random.randint(own_key, (), max(1, total - bound), min(bound, total - 1) + 1)
        return jnp.stack([one, total - one])
    lengths = jnp.asarray(length_profile(number_of, total, bound, slope), jnp.int32)
    pairs = (number_of - 1) // 2
    source_of, taker = lengths[1:1 + 2 * pairs:2], lengths[2:2 + 2 * pairs:2]
    room = jnp.minimum(source_of - 1, bound - taker)
    shifted = jax.random.randint(jax.random.fold_in(own_key, 1), (pairs,), 0, 1 << 20) % (room + 1)
    lengths = lengths.at[1:1 + 2 * pairs:2].set(source_of - shifted).at[2:2 + 2 * pairs:2].set(taker + shifted)
    return lengths[jax.random.permutation(jax.random.fold_in(own_key, 2), number_of)]


def deal_out(rng, own, number, rows, count, top, most, lean):
    order = jax.random.permutation(rng, count)
    crowded, usual = shares(count, rows * top, most, lean, True), shares(count, rows * top, most, lean, False)
    places = jnp.arange(count)

    def named(lengths, turn):
        used = int((lengths > 0).sum())
        fixed = max(1, used // 4)
        passed = fixed + (places - fixed + turn * (used - fixed)) % max(1, count - fixed)
        return jnp.zeros((count,), jnp.int32).at[order[jnp.where(places < fixed, places, passed)]].set(jnp.asarray(lengths, jnp.int32))

    lengths = jnp.where(number % 4 == 0, named(crowded, number // 4), named(usual, number - number // 4 - 1))
    mixed = jax.random.permutation(jax.random.fold_in(own, 3), count)
    giver, sink = mixed[0:count // 2 * 2:2], mixed[1:count // 2 * 2:2]
    slack = jnp.minimum(lengths[giver] - 1, most - lengths[sink]) // 2
    slack = jnp.where((giver == order[0]) | (sink == order[0]) | (lengths[sink] == 0), 0, jnp.maximum(slack, 0))
    passed = jax.random.randint(jax.random.fold_in(own, 4), (count // 2,), 0, 1 << 20) % (slack + 1)
    lengths = lengths.at[giver].add(-passed).at[sink].add(passed)
    items = jnp.searchsorted(jnp.cumsum(lengths), jnp.arange(rows * top), side="right").astype(jnp.int32)
    listing = items.reshape(top, rows).T
    listing = listing[jax.random.permutation(jax.random.fold_in(own, 1), rows)]
    turn = jax.random.randint(jax.random.fold_in(own, 2), (rows, 1), 0, top)
    return jnp.take_along_axis(listing, (jnp.arange(top)[None, :] + turn) % top, axis=1)


def shares(count, total, bound, lean, full):
    portions = [(1 << 20) // math.isqrt(standing ** lean) + 1 for standing in range(1, count + 1)]
    largest = bound if full else min(bound, max(-(-total // count), total * portions[0] // sum(portions)))
    least = 1 if total - largest >= count - 1 else 0
    holding, spare = [largest] + [least] * (count - 1), total - largest - least * (count - 1)
    while spare > 0:
        free = [i for i in range(1, count) if holding[i] < largest] or [i for i in range(1, count) if holding[i] < bound]
        whole, left = sum([portions[i] for i in free]), spare
        for i in free:
            extra = min(bound - holding[i], max(1, left * portions[i] // whole), spare)
            holding[i] = holding[i] + extra
            spare = spare - extra
    return np.array(holding)


def scatter_about(own_key, extent, deviation, reach, shards=(), held_as=jnp.bfloat16):
    loudness = steps_of(own_key, extent, shards, -0.22, 0.18) if shards else 1.0
    values = jax.random.normal(own_key, extent, jnp.float32) * deviation * loudness
    return jnp.minimum(jnp.maximum(values, -reach), reach).astype(held_as)


def setup_inputs(seed: int = 0) -> dict:
    key_of = jax.random.split(jax.random.key(seed), 15)
    inputs = scatter_about(key_of[0], (MICRO, TOKENS, D), 1.0, 6.0, ((1, 4),))
    cotangent = scatter_about(key_of[1], (MICRO, TOKENS, D), 1.0, 6.0, ((1, 4),))
    attn_gain = jnp.clip(1.0 + 0.1 * jax.random.normal(key_of[2], (SECTIONS, D), jnp.float32), 0.5, 1.5).astype(jnp.bfloat16)
    query_weight = scatter_about(key_of[3], (SECTIONS, D, D), D ** -0.5, 0.21875, ((0, 2), (1, 4), (2, 4)))
    key_weight = scatter_about(key_of[4], (SECTIONS, D, D), D ** -0.5, 0.21875, ((0, 2), (1, 4), (2, 4)))
    value_weight = scatter_about(key_of[5], (SECTIONS, D, D), D ** -0.5, 0.21875, ((0, 2), (1, 4), (2, 4)))
    out_weight = scatter_about(key_of[6], (SECTIONS, D, D), (D // 64) ** -0.5, 1.75, ((0, 2), (1, 4), (2, 4)))
    rel_table = scatter_about(key_of[7], (SECTIONS, BUCKETS, HEADS), 1.0, 4.0, ((0, 2), (1, 4), (2, 4)))
    ffn_gain = jnp.clip(1.0 + 0.1 * jax.random.normal(key_of[8], (SECTIONS, D), jnp.float32), 0.5, 1.5).astype(jnp.bfloat16)
    router_weight = scatter_about(key_of[9], (SECTIONS, D, EXPERTS), (2 * D) ** -0.5, 0.15625, ((0, 2), (1, 4)))
    expert_in = scatter_about(key_of[10], (SECTIONS, EXPERTS, D, FF), D ** -0.5, 0.21875, ((0, 2), (1, 4), (3, 4)))
    expert_out = scatter_about(key_of[11], (SECTIONS, EXPERTS, FF, D), (max(1, 2 * FF // (5 * EXPERTS * EXPERTS))) ** -0.5, 0.625, ((0, 2), (1, 4), (2, 4)))
    routes_keys = jax.random.split(jax.random.fold_in(key_of[12], 1), SECTIONS * MICRO * TOKENS // SEQ)
    routes_turns = jax.random.permutation(jax.random.fold_in(key_of[12], 3), SECTIONS * MICRO * TOKENS // SEQ)
    routes = jax.vmap(lambda own, number: deal_out(jax.random.fold_in(key_of[12], 2), own, number, SEQ, EXPERTS, 1, CAP, 1))(routes_keys, routes_turns).reshape((SECTIONS, MICRO, TOKENS, 1))
    segments = jax.vmap(lambda own: jnp.searchsorted(jnp.cumsum(ragged_sizes(own, 4 * N_EXPERT, TOKENS, SEQ // 2, 1)), jnp.arange(TOKENS), side="right"))(jax.random.split(key_of[13], MICRO)).reshape((MICRO, TOKENS)).astype(jnp.int32)
    return {"inputs": inputs, "cotangent": cotangent, "attn_gain": attn_gain, "query_weight": query_weight, "key_weight": key_weight, "value_weight": value_weight, "out_weight": out_weight, "rel_table": rel_table, "ffn_gain": ffn_gain, "router_weight": router_weight, "expert_in": expert_in, "expert_out": expert_out, "routes": routes, "segments": segments}


@jax.custom_vjp
def low(v):
    return lax.optimization_barrier(v.astype(jnp.bfloat16)).astype(jnp.float32)

@jax.custom_vjp
def low_back(v):
    return v

def low_keep(v):
    return (low(v), None)

def low_pass(kept, grad):
    return (grad,)

def back_keep(v):
    return (v, None)

def back_low(kept, grad):
    return (low(grad),)
low.defvjp(low_keep, low_pass)
low_back.defvjp(back_keep, back_low)

def both_ways(values):
    return low_back(low(values))

def bucket_ids(length):
    half_count = BUCKETS // 2
    exact_count = half_count // 2
    places = jnp.arange(length, dtype=jnp.int32)
    offsets = places[None, :] - places[:, None]
    distance = jnp.abs(offsets)
    larger = jnp.full_like(distance, exact_count)
    for level_index in range(1, half_count - exact_count):
        border = int(math.ceil(exact_count * (128.0 / exact_count) ** (level_index / (half_count - exact_count)) - 1e-09))
        larger = larger + (distance >= border).astype(jnp.int32)
    bucket = jnp.where(distance < exact_count, distance, larger)
    return (bucket + jnp.where(offsets > 0, half_count, 0)).astype(jnp.int32)

def rms_scale(values, gain_vector):
    return values * lax.rsqrt(lax.optimization_barrier(jnp.mean(values * values, axis=-1, keepdims=True)) + 1e-06) * gain_vector

def attend(query_heads, key_heads, value_heads, labels, rel_bias):
    scores = jnp.einsum('qhe,khe->hqk', query_heads, key_heads, precision=lax.Precision.HIGHEST) * HEAD_DIM ** (-0.5) + rel_bias
    scores = low_back(scores)
    same_doc = labels[:, None] == labels[None, :]
    scores = jnp.where(same_doc[None], scores, -1000000000.0)
    weights = jax.nn.softmax(scores, axis=-1)
    mixed_heads = jnp.einsum('hqk,khe->qhe', low(weights), value_heads, precision=lax.Precision.HIGHEST)
    return both_ways(mixed_heads)

def run_expert(packed):
    rows, weight_in, weight_out = packed
    hidden = low_back(jnp.dot(rows, weight_in, precision=lax.Precision.HIGHEST))
    active = low(jax.nn.gelu(hidden))
    return both_ways(jnp.dot(active, weight_out, precision=lax.Precision.HIGHEST))

def encoder_layer(layer_in, params, route_ids, labels, buckets):
    gain_one, query_matrix, key_matrix, value_matrix, attn_out_weight, bias_table, gain_two, router_matrix, weight_in, weight_out = params
    token_count = layer_in.shape[0]
    normed = low(rms_scale(layer_in, gain_one))
    query_heads = both_ways(jnp.dot(normed, query_matrix, precision=lax.Precision.HIGHEST)).reshape(N_EXPERT, SEQ, HEADS, HEAD_DIM)
    key_heads = both_ways(jnp.dot(normed, key_matrix, precision=lax.Precision.HIGHEST)).reshape(N_EXPERT, SEQ, HEADS, HEAD_DIM)
    value_heads = both_ways(jnp.dot(normed, value_matrix, precision=lax.Precision.HIGHEST)).reshape(N_EXPERT, SEQ, HEADS, HEAD_DIM)
    rel_bias = jnp.transpose(bias_table[buckets], (2, 0, 1))

    def one_sequence(packed):
        return attend(packed[0], packed[1], packed[2], packed[3], rel_bias)
    mixed_heads = lax.map(jax.checkpoint(one_sequence), (query_heads, key_heads, value_heads, labels.reshape(N_EXPERT, SEQ)))
    attn_value = low_back(jnp.dot(mixed_heads.reshape(token_count, D), attn_out_weight.T, precision=lax.Precision.HIGHEST))
    residual = layer_in + attn_value
    normed_two = rms_scale(residual, gain_two)
    logits = jnp.dot(normed_two, router_matrix, precision=lax.Precision.HIGHEST)
    router_probs = jax.nn.softmax(logits, axis=-1)
    picked = route_ids[:, 0]
    chosen = picked[:, None] == jnp.arange(EXPERTS, dtype=jnp.int32)[None, :]
    gate_value = lax.optimization_barrier(jnp.sum(jnp.where(chosen, router_probs, 0.0), axis=-1, keepdims=True))
    counts = jnp.cumsum(chosen.astype(jnp.int32).reshape(N_EXPERT, SEQ, EXPERTS), axis=1).astype(jnp.int32)
    counts = counts.reshape(token_count, EXPERTS)
    slot_number = (lax.optimization_barrier(jnp.sum(jnp.where(chosen, counts, 0), axis=-1)) - 1).astype(jnp.int32)
    owner_index = (jnp.arange(token_count, dtype=jnp.int32) // SEQ).astype(jnp.int32)
    slot_index = (picked * (N_EXPERT * CAP) + owner_index * CAP + slot_number).astype(jnp.int32)
    rows = both_ways(normed_two)
    buffer = jnp.zeros((EXPERTS * N_EXPERT * CAP, D), jnp.float32).at[slot_index].set(rows)
    results = lax.map(jax.checkpoint(run_expert), (buffer.reshape(EXPERTS, N_EXPERT * CAP, D), weight_in, weight_out))
    expert_value = results.reshape(EXPERTS * N_EXPERT * CAP, D)[slot_index]
    return residual + gate_value * expert_value

def reference(inputs, cotangent, attn_gain, query_weight, key_weight, value_weight, out_weight, rel_table, ffn_gain, router_weight, expert_in, expert_out, routes, segments):
    buckets = bucket_ids(SEQ)
    floats = [array.astype(jnp.float32) for array in (attn_gain, query_weight, key_weight, value_weight, out_weight, rel_table, ffn_gain, router_weight, expert_in, expert_out)]
    start_float = inputs.astype(jnp.float32)

    def forward(deltas, *params):
        finals = []
        sectioned = [[] for section_index in range(N_SECTION)]
        for micro_index in range(MICRO):
            current = start_float[micro_index] + deltas[0, micro_index]
            for section_index in range(N_SECTION):
                if section_index > 0:
                    current = both_ways(current) + deltas[section_index, micro_index]
                layer_params = [param[section_index] for param in params]
                current = encoder_layer(current, layer_params, routes[section_index, micro_index], segments[micro_index], buckets)
                sectioned[section_index].append(current)
            finals.append(current)
        return (jnp.stack(finals), jnp.stack([jnp.stack(entry) for entry in sectioned]))
    deltas = jnp.zeros((N_SECTION, MICRO, TOKENS, D), jnp.float32)
    finals, pullback, sectioned = jax.vjp(forward, deltas, *floats, has_aux=True)
    grads = pullback(cotangent.astype(jnp.float32))
    return (sectioned.astype(jnp.bfloat16), grads[0].astype(jnp.bfloat16), grads[1], grads[2], grads[3], grads[4], grads[5], grads[6], grads[7], grads[8], grads[9], grads[10])
```

```python
import math

import jax
import jax.numpy as jnp
from jax import lax
from jax.experimental import pallas as pl
from jax.experimental.pallas import tpu as pltpu
from jax.sharding import PartitionSpec as P

BUCKETS = 32


PEERS = 4
MESH = pl.DeviceIdType.MESH


def use_kernels():
    return (
        lax.axis_size("expert") == PEERS
        and lax.axis_size("tensor") == PEERS
        and lax.axis_size("section") == 2
    )


def around(axis, distance):
    return lax.rem(lax.axis_index(axis) + distance, PEERS)


def greet(axes, sibling=False):
    barrier = pltpu.get_barrier_semaphore()
    count = 0
    for axis in axes:
        for distance in range(1, PEERS):
            pl.semaphore_signal(
                barrier, inc=1, device_id={axis: around(axis, distance)}, device_id_type=MESH
            )
            count += 1
    if sibling:
        pl.semaphore_signal(
            barrier,
            inc=1,
            device_id={"section": 1 - lax.axis_index("section")},
            device_id_type=MESH,
        )
        count += 1
    pl.semaphore_wait(barrier, count)


def send(source, target, sends, receives, slot, axis, peer):
    copy = pltpu.make_async_remote_copy(
        src_ref=source,
        dst_ref=target,
        send_sem=sends.at[slot],
        recv_sem=receives.at[slot],
        device_id={axis: peer},
        device_id_type=MESH,
    )
    copy.start()
    return copy


def params(number):
    return pltpu.CompilerParams(
        collective_id=number, has_side_effects=True, vmem_limit_bytes=40 * 1024 * 1024
    )


def sems(count):
    return [pltpu.SemaphoreType.DMA((count,)), pltpu.SemaphoreType.DMA((count,))]


VMEM = pl.BlockSpec(memory_space=pltpu.VMEM)
ANY = pl.BlockSpec(memory_space=pl.ANY)


def start_kernel(
    attn, small, ids, first, second,
    attn_all, small_all, ids_all, first_all, second_all,
    near_send, near_recv, far_send, far_recv, pass_send, pass_recv, here,
):
    section = lax.axis_index("section")
    expert = lax.axis_index("expert")
    other = 1 - section
    greet(["expert"], sibling=True)
    far = []
    for distance in range(1, PEERS):
        peer = around("expert", distance)
        far.append([
            send(attn, attn_all.at[section, expert], far_send, far_recv, 2 * distance - 2, "expert", peer),
            send(small, small_all.at[section, expert], far_send, far_recv, 2 * distance - 1, "expert", peer),
        ])
    pairs = [
        (attn, attn_all.at[section, expert]),
        (small, small_all.at[section, expert]),
        (ids, ids_all.at[section]),
        (first, first_all.at[section]),
        (second, second_all.at[section]),
    ]
    near = []
    own = []
    for slot, (source, target) in enumerate(pairs):
        near.append(send(source, target, near_send, near_recv, slot, "section", other))
        copy = pltpu.make_async_copy(source, target, here.at[slot])
        copy.start()
        own.append(copy)
    passed = []
    for distance in range(1, PEERS):
        origin = around("expert", PEERS - distance)
        for copy in far[distance - 1]:
            copy.wait_recv()
        for which, whole in enumerate((attn_all, small_all)):
            place = whole.at[section, origin]
            passed.append(
                send(place, place, pass_send, pass_recv, 2 * distance - 2 + which, "section", other)
            )
    for copy in own:
        copy.wait()
    for copy in near + passed:
        copy.wait()
    for group in far:
        for copy in group:
            copy.wait_send()


def collect_weights(attn, small, ids, first, second):
    if not use_kernels():
        over = lambda a: lax.all_gather(a, "section")
        return (
            over(lax.all_gather(attn, "expert")),
            over(lax.all_gather(small, "expert")),
            over(ids),
            over(first),
            over(second),
        )
    shapes = [
        (2, PEERS) + attn.shape,
        (2, PEERS) + small.shape,
        (2,) + ids.shape,
        (2,) + first.shape,
        (2,) + second.shape,
    ]
    return pl.pallas_call(
        start_kernel,
        out_shape=[jax.ShapeDtypeStruct(shape, jnp.bfloat16) for shape in shapes],
        in_specs=[ANY] * 5,
        out_specs=[ANY] * 5,
        scratch_shapes=sems(5) + sems(6) + sems(6) + [pltpu.SemaphoreType.DMA((5,))],
        compiler_params=params(1),
    )(attn, small, ids, first, second)


def total_kernel(part, whole, landed, send_one, recv_one, send_two, recv_two):
    own = lax.axis_index("tensor")
    greet(["tensor"])
    one = []
    for distance in range(1, PEERS):
        peer = around("tensor", distance)
        one.append(
            send(part.at[peer], landed.at[distance - 1], send_one, recv_one, distance - 1, "tensor", peer)
        )
    total = part[own].astype(jnp.float32)
    for slot, copy in enumerate(one):
        copy.wait_recv()
        total = total + landed[slot].astype(jnp.float32)
    whole[own] = total.astype(whole.dtype)
    two = []
    for distance in range(1, PEERS):
        peer = around("tensor", distance)
        two.append(
            send(whole.at[own], whole.at[own], send_two, recv_two, distance - 1, "tensor", peer)
        )
    for copy in two:
        copy.wait()
    for copy in one:
        copy.wait_send()


def sum_heads(part):
    if not use_kernels():
        return lax.psum(part, "tensor")
    length, width = part.shape
    split = part.reshape(PEERS, length // PEERS, width)
    return pl.pallas_call(
        total_kernel,
        out_shape=jax.ShapeDtypeStruct(split.shape, split.dtype),
        in_specs=[VMEM],
        out_specs=VMEM,
        scratch_shapes=[pltpu.VMEM((PEERS - 1,) + split.shape[1:], split.dtype)] + sems(3) + sems(3),
        compiler_params=params(2),
    )(split).reshape(length, width)


def dispatch_kernel(rows, whole, send_one, recv_one, send_two, recv_two):
    own = lax.axis_index("tensor")
    expert = lax.axis_index("expert")
    greet(["tensor", "expert"])
    one = []
    for distance in range(1, PEERS):
        peer = around("expert", distance)
        one.append(
            send(rows.at[peer], whole.at[own, expert], send_one, recv_one, distance - 1, "expert", peer)
        )
    whole[own, expert] = rows[expert]
    for copy in one:
        copy.wait_recv()
    two = []
    for distance in range(1, PEERS):
        peer = around("tensor", distance)
        two.append(
            send(whole.at[own], whole.at[own], send_two, recv_two, distance - 1, "tensor", peer)
        )
    for copy in two:
        copy.wait()
    for copy in one:
        copy.wait_send()


def dispatch(rows):
    if not use_kernels():
        arrived = lax.all_to_all(rows, "expert", split_axis=0, concat_axis=0, tiled=True)
        return lax.all_gather(arrived, "tensor")
    return pl.pallas_call(
        dispatch_kernel,
        out_shape=jax.ShapeDtypeStruct((PEERS,) + rows.shape, rows.dtype),
        in_specs=[VMEM],
        out_specs=VMEM,
        scratch_shapes=sems(3) + sems(3),
        compiler_params=params(3),
    )(rows)


def combine_kernel(
    part, pick, whole, landed, reduced, arrived,
    send_one, recv_one, send_two, recv_two, send_three, recv_three,
):
    own = lax.axis_index("tensor")
    expert = lax.axis_index("expert")
    greet(["tensor", "expert"])
    one = []
    for distance in range(1, PEERS):
        peer = around("tensor", distance)
        one.append(
            send(part.at[peer], landed.at[distance - 1], send_one, recv_one, distance - 1, "tensor", peer)
        )
    for copy in one:
        copy.wait_recv()
    total = part[own].astype(jnp.float32)
    for slot in range(PEERS - 1):
        total = total + landed[slot].astype(jnp.float32)
    reduced[...] = total.astype(reduced.dtype)
    two = []
    for distance in range(1, PEERS):
        peer = around("expert", distance)
        two.append(
            send(reduced.at[peer], arrived.at[expert], send_two, recv_two, distance - 1, "expert", peer)
        )
    arrived[expert] = reduced[expert]
    for copy in two:
        copy.wait_recv()
    groups, capacity, width = arrived.shape
    whole[own] = jnp.dot(
        pick[...],
        arrived[...].reshape(groups * capacity, width),
        preferred_element_type=jnp.float32,
    ).astype(whole.dtype)
    three = []
    for distance in range(1, PEERS):
        peer = around("tensor", distance)
        three.append(
            send(whole.at[own], whole.at[own], send_three, recv_three, distance - 1, "tensor", peer)
        )
    for copy in three:
        copy.wait()
    for copy in one + two:
        copy.wait_send()


def combine(part, pick):
    if use_kernels():
        block = part.shape[1:]
        whole = pl.pallas_call(
            combine_kernel,
            out_shape=jax.ShapeDtypeStruct((PEERS, pick.shape[0], part.shape[3]), part.dtype),
            in_specs=[VMEM, VMEM],
            out_specs=VMEM,
            scratch_shapes=[
                pltpu.VMEM((PEERS - 1,) + block, part.dtype),
                pltpu.VMEM(block, part.dtype),
                pltpu.VMEM(block, part.dtype),
            ]
            + sems(3)
            + sems(3)
            + sems(3),
            compiler_params=params(4),
        )(part, pick)
    else:
        share = lax.psum_scatter(part, "tensor", scatter_dimension=0, tiled=False)
        returned = lax.all_to_all(share, "expert", split_axis=0, concat_axis=0, tiled=True)
        picked = jnp.dot(
            pick, returned.reshape(-1, part.shape[3]), preferred_element_type=jnp.float32
        ).astype(part.dtype)
        whole = lax.all_gather(picked, "tensor")
    return jnp.swapaxes(whole, 0, 1).reshape(pick.shape[0], -1)


def finish_kernel(
    grads, small, grads_out, small_out, landed, landed_small, send_one, recv_one
):
    expert = lax.axis_index("expert")
    greet(["expert"])
    copies = []
    for distance in range(1, PEERS):
        peer = around("expert", distance)
        slot = distance - 1
        copies.append([
            send(grads.at[peer], landed.at[slot], send_one, recv_one, 2 * slot, "expert", peer),
            send(small.at[peer], landed_small.at[slot], send_one, recv_one, 2 * slot + 1, "expert", peer),
        ])
    grads_out[...] = grads[expert].astype(jnp.float32)
    small_out[...] = small[expert].astype(jnp.float32)
    for slot, group in enumerate(copies):
        for copy in group:
            copy.wait_recv()
        grads_out[...] += landed[slot].astype(jnp.float32)
        small_out[...] += landed_small[slot].astype(jnp.float32)
    for group in copies:
        for copy in group:
            copy.wait_send()


def reduce_grads(grads, small):
    if not use_kernels():
        return tuple(
            lax.psum_scatter(part, "expert", scatter_dimension=0, tiled=False).astype(jnp.float32)
            for part in (grads, small)
        )
    return pl.pallas_call(
        finish_kernel,
        out_shape=[
            jax.ShapeDtypeStruct(grads.shape[1:], jnp.float32),
            jax.ShapeDtypeStruct(small.shape[1:], jnp.float32),
        ],
        in_specs=[VMEM] * 2,
        out_specs=[VMEM] * 2,
        scratch_shapes=[
            pltpu.VMEM((PEERS - 1,) + grads.shape[1:], grads.dtype),
            pltpu.VMEM((PEERS - 1,) + small.shape[1:], small.dtype),
        ]
        + sems(6),
        compiler_params=params(5),
    )(grads, small)


def own_features(rows):
    width = rows.shape[1] // lax.axis_size("tensor")
    return lax.dynamic_slice_in_dim(rows, lax.axis_index("tensor") * width, width, 1)


def slots_for(length, experts):
    capacity = 5 * length // (4 * experts)
    return -(-capacity // 16) * 16


def offset_buckets(length):
    half_count = BUCKETS // 2
    exact_count = half_count // 2
    offsets = jnp.arange(2 * length, dtype=jnp.int32) - (length - 1)
    distance = jnp.abs(offsets)
    larger = jnp.full_like(distance, exact_count)
    for level_index in range(1, half_count - exact_count):
        border = int(
            math.ceil(
                exact_count * (128.0 / exact_count) ** (level_index / (half_count - exact_count))
                - 1e-09
            )
        )
        larger = larger + (distance >= border).astype(jnp.int32)
    bucket = jnp.where(distance < exact_count, distance, larger)
    return bucket + jnp.where(offsets > 0, half_count, 0)


def spread_offsets(per_offset, length):
    heads_here = per_offset.shape[0]
    tiled = jnp.tile(per_offset, (1, length))[:, : length * (2 * length - 1)]
    skewed = tiled.reshape(heads_here, length, 2 * length - 1)
    return skewed[:, :, length - 1 :]


def collect_offsets(grid_values, length):
    heads_here = grid_values.shape[0]
    padded = jnp.pad(grid_values, ((0, 0), (0, 0), (length - 1, 0)))
    flat = jnp.pad(padded.reshape(heads_here, length * (2 * length - 1)), ((0, 0), (0, length)))
    return jnp.sum(flat.reshape(heads_here, length, 2 * length), axis=1, dtype=jnp.float32)


def rms_scale(values, gain_vector):
    return (
        values * lax.rsqrt(jnp.mean(values * values, axis=-1, keepdims=True) + 1e-06) * gain_vector
    )


def slot_places(route_ids, experts, capacity):
    chosen = route_ids[:, None] == jnp.arange(experts, dtype=jnp.int32)[None, :]
    counts = jnp.cumsum(chosen.astype(jnp.int32), axis=0)
    slot_number = jnp.sum(jnp.where(chosen, counts, 0), axis=-1) - 1
    return (chosen, route_ids * capacity + slot_number)


def position_bias(offset_table, bias_table, length):
    per_offset = jnp.dot(
        offset_table, bias_table.astype(jnp.float32), precision=lax.Precision.HIGHEST
    )
    return spread_offsets(per_offset.T, length)


def attention_probs(query_heads, key_heads, rel_bias, labels, head_size):
    scores = (
        jnp.einsum("qhe,khe->hqk", query_heads, key_heads, preferred_element_type=jnp.float32)
        * head_size ** (-0.5)
        + rel_bias
    )
    same_doc = labels[:, None] == labels[None, :]
    return jnp.where(same_doc[None], scores, -1000000000.0)


def join_rows(arrived):
    parts, experts, capacity, width = arrived.shape
    return jnp.transpose(arrived, (1, 2, 0, 3)).reshape(experts * capacity, parts * width)


def split_rows(rows, shape):
    parts, experts, capacity, width = shape
    return jnp.transpose(rows.reshape(experts, capacity, parts, width), (2, 0, 1, 3))


def forward_layer(layer_in, weights, route_ids, labels, offset_table, weight_in, weight_out):
    gain_one, joint_weight, attn_out_weight, bias_table, gain_two, router_matrix = weights
    length, model_width = layer_in.shape
    heads_here = bias_table.shape[1]
    head_size = attn_out_weight.shape[1] // heads_here
    experts = router_matrix.shape[1]
    capacity = slots_for(length, experts)
    input_float = layer_in.astype(jnp.float32)
    normed = rms_scale(input_float, gain_one).astype(jnp.bfloat16)
    joint_heads = jnp.dot(normed, joint_weight, preferred_element_type=jnp.float32).astype(
        jnp.bfloat16
    )
    query_heads, key_heads, value_heads = [
        part.reshape(length, heads_here, head_size) for part in jnp.split(joint_heads, 3, axis=1)
    ]
    rel_bias = position_bias(offset_table, bias_table, length)
    scores = attention_probs(query_heads, key_heads, rel_bias, labels, head_size)
    log_total = jax.nn.logsumexp(scores, axis=-1)
    probs_low = jnp.exp(scores - log_total[..., None]).astype(jnp.bfloat16)
    mixed_heads = (
        jnp.einsum("hqk,khe->qhe", probs_low, value_heads, preferred_element_type=jnp.float32)
        .astype(jnp.bfloat16)
        .reshape(length, heads_here * head_size)
    )
    partial_out = lax.dot_general(
        mixed_heads, attn_out_weight, (((1,), (1,)), ((), ())), preferred_element_type=jnp.float32
    )
    residual = input_float + sum_heads(partial_out.astype(jnp.bfloat16)).astype(jnp.float32)
    normed_two = rms_scale(residual, gain_two)
    logits = jnp.dot(normed_two, router_matrix, precision=lax.Precision.HIGHEST)
    router_probs = jax.nn.softmax(logits, axis=-1)
    chosen, slot_index = slot_places(route_ids, experts, capacity)
    gate_value = jnp.sum(jnp.where(chosen, router_probs, 0.0), axis=-1, keepdims=True)
    pick = (
        slot_index[:, None] == jnp.arange(experts * capacity, dtype=jnp.int32)[None, :]
    ).astype(jnp.bfloat16)
    buffer = lax.dot_general(
        pick,
        own_features(normed_two).astype(jnp.bfloat16),
        (((0,), (0,)), ((), ())),
        preferred_element_type=jnp.float32,
    ).astype(jnp.bfloat16)
    arrived = dispatch(buffer.reshape(experts, capacity, -1))
    groups = join_rows(arrived)
    hidden = jnp.dot(groups, weight_in, preferred_element_type=jnp.float32)
    active = jax.nn.gelu(hidden).astype(jnp.bfloat16)
    partial_rows = jnp.dot(active, weight_out, preferred_element_type=jnp.float32)
    expert_low = combine(split_rows(partial_rows.astype(jnp.bfloat16), arrived.shape), pick)
    output = (residual + gate_value * expert_low.astype(jnp.float32)).astype(jnp.bfloat16)
    kept_state = (
        layer_in,
        normed,
        query_heads,
        key_heads,
        value_heads,
        mixed_heads,
        log_total,
        residual,
        router_probs,
        gate_value,
        pick,
        arrived.shape,
        groups,
        hidden,
        active,
        expert_low,
    )
    return (output, kept_state)


def backward_layer(
    grad_out, kept_state, weights, route_ids, labels, offset_table, weight_in, weight_out
):
    (
        layer_in,
        normed,
        query_heads,
        key_heads,
        value_heads,
        mixed_heads,
        log_total,
        residual,
        router_probs,
        gate_value,
        pick,
        arrived_shape,
        groups,
        hidden,
        active,
        expert_low,
    ) = kept_state
    gain_one, joint_weight, attn_out_weight, bias_table, gain_two, router_matrix = weights
    length, model_width = layer_in.shape
    heads_here = bias_table.shape[1]
    head_size = attn_out_weight.shape[1] // heads_here
    experts = router_matrix.shape[1]
    capacity = slots_for(length, experts)
    grad_float = grad_out.astype(jnp.float32)
    grad_gate = jnp.sum(grad_float * expert_low.astype(jnp.float32), axis=-1, keepdims=True)
    grad_value = (gate_value * grad_float).astype(jnp.bfloat16)
    grad_buffer = lax.dot_general(
        pick, own_features(grad_value), (((0,), (0,)), ((), ())), preferred_element_type=jnp.float32
    ).astype(jnp.bfloat16)
    grad_groups = join_rows(dispatch(grad_buffer.reshape(experts, capacity, -1)))
    grad_active = lax.dot_general(
        grad_groups, weight_out, (((1,), (1,)), ((), ())), preferred_element_type=jnp.float32
    )
    grad_weight_out = lax.dot_general(
        active, grad_groups, (((0,), (0,)), ((), ())), preferred_element_type=jnp.float32
    )
    gelu_pull = jax.vjp(jax.nn.gelu, hidden)[1]
    grad_hidden = gelu_pull(grad_active)[0].astype(jnp.bfloat16)
    grad_weight_in = lax.dot_general(
        groups, grad_hidden, (((0,), (0,)), ((), ())), preferred_element_type=jnp.float32
    )
    grad_partial = lax.dot_general(
        grad_hidden, weight_in, (((1,), (1,)), ((), ())), preferred_element_type=jnp.float32
    )
    grad_normed_two = combine(
        split_rows(grad_partial.astype(jnp.bfloat16), arrived_shape), pick
    ).astype(jnp.float32)
    chosen = route_ids[:, None] == jnp.arange(experts, dtype=jnp.int32)[None, :]
    grad_logits = grad_gate * gate_value * (chosen.astype(jnp.float32) - router_probs)
    grad_normed_two = grad_normed_two + lax.dot_general(
        grad_logits, router_matrix, (((1,), (1,)), ((), ())), precision=lax.Precision.HIGHEST
    )
    normed_two, norm_pull = jax.vjp(rms_scale, residual, gain_two)
    grad_router = lax.dot_general(
        normed_two, grad_logits, (((0,), (0,)), ((), ())), precision=lax.Precision.HIGHEST
    )
    grad_residual, grad_gain_two = norm_pull(grad_normed_two)
    grad_residual = grad_residual + grad_float
    grad_attn = grad_residual.astype(jnp.bfloat16)
    grad_attn_out = lax.dot_general(
        grad_attn, mixed_heads, (((0,), (0,)), ((), ())), preferred_element_type=jnp.float32
    )
    grad_mixed = (
        jnp.dot(grad_attn, attn_out_weight, preferred_element_type=jnp.float32)
        .astype(jnp.bfloat16)
        .reshape(length, heads_here, head_size)
    )
    rel_bias = position_bias(offset_table, bias_table, length)
    scores = attention_probs(query_heads, key_heads, rel_bias, labels, head_size)
    probs_float = jnp.exp(scores - log_total[..., None])
    probs_low = probs_float.astype(jnp.bfloat16)
    grad_probs = jnp.einsum(
        "qhe,khe->hqk", grad_mixed, value_heads, preferred_element_type=jnp.float32
    )
    grad_scores = (
        probs_float * (grad_probs - jnp.sum(probs_float * grad_probs, axis=-1, keepdims=True))
    ).astype(jnp.bfloat16)
    grad_query = (
        jnp.einsum("hqk,khe->qhe", grad_scores, key_heads, preferred_element_type=jnp.float32)
        * head_size ** (-0.5)
    ).astype(jnp.bfloat16)
    grad_keys = (
        jnp.einsum("hqk,qhe->khe", grad_scores, query_heads, preferred_element_type=jnp.float32)
        * head_size ** (-0.5)
    ).astype(jnp.bfloat16)
    grad_values = jnp.einsum(
        "hqk,qhe->khe", probs_low, grad_mixed, preferred_element_type=jnp.float32
    ).astype(jnp.bfloat16)
    offset_sums = collect_offsets(grad_scores, length)
    grad_table = jnp.einsum("kb,hk->bh", offset_table, offset_sums, precision=lax.Precision.HIGHEST)
    grad_joint = jnp.concatenate(
        [
            part.reshape(length, heads_here * head_size)
            for part in (grad_query, grad_keys, grad_values)
        ],
        axis=1,
    )
    grad_joint_weight = lax.dot_general(
        normed, grad_joint, (((0,), (0,)), ((), ())), preferred_element_type=jnp.float32
    )
    grad_normed_part = lax.dot_general(
        grad_joint, joint_weight, (((1,), (1,)), ((), ())), preferred_element_type=jnp.float32
    )
    grad_normed = sum_heads(grad_normed_part.astype(jnp.bfloat16)).astype(jnp.float32)
    input_pull = jax.vjp(rms_scale, layer_in.astype(jnp.float32), gain_one)[1]
    grad_input_part, grad_gain_one = input_pull(grad_normed)
    grad_input = (grad_residual + grad_input_part).astype(jnp.bfloat16)
    attn_terms = (
        grad_gain_one,
        grad_joint_weight,
        grad_attn_out,
        grad_table,
        grad_gain_two,
        grad_router,
    )
    return (grad_input, attn_terms, (grad_weight_in, grad_weight_out))


def pack_terms(attn_terms, expert_count):
    gain_one, joint, attn_out, table, gain_two, router = attn_terms
    width = gain_one.shape[0]
    piece = width // expert_count
    columns = attn_out.shape[1]
    matrices = jnp.stack(
        [part.reshape(expert_count, piece, columns) for part in jnp.split(joint, 3, axis=1)]
        + [attn_out.reshape(expert_count, piece, columns)],
        axis=1,
    )
    rows = table.shape[0] // expert_count
    table = jnp.pad(
        table.reshape(expert_count, rows, -1), ((0, 0), (0, piece - rows), (0, 0))
    ).reshape(width, -1)
    used = 2 + table.shape[1] + router.shape[1]
    small = jnp.concatenate(
        [
            gain_one[:, None],
            gain_two[:, None],
            table,
            router,
            jnp.zeros((width, 128 - used), jnp.float32),
        ],
        axis=1,
    ).reshape(expert_count, piece, 128)
    return (matrices, small)


def swap_micro(per_layer):
    section = lax.axis_index("section")
    own = jnp.where(section == 0, per_layer[0], per_layer[1])
    other = jnp.where(section == 0, per_layer[1], per_layer[0])
    came = lax.ppermute(other, "section", [(0, 1), (1, 0)])
    return jnp.where(
        section == 0, jnp.stack([own, came]), jnp.stack([came, own])
    )[None]


def local(
    inputs,
    cotangent,
    attn_gain,
    query_weight,
    key_weight,
    value_weight,
    out_weight,
    rel_table,
    ffn_gain,
    router_weight,
    expert_in,
    expert_out,
    routes,
    segments,
):
    section = lax.axis_index("section")
    layers = lax.axis_size("section")
    expert_count = lax.axis_size("expert")
    micro_count, length, model_width = inputs.shape
    heads_here = rel_table.shape[2]
    experts = router_weight.shape[2]
    piece = attn_gain.shape[1]
    attn = jnp.concatenate([query_weight, key_weight, value_weight, out_weight], axis=0)
    used = 2 + heads_here + experts
    small = jnp.concatenate(
        [
            attn_gain[0][:, None],
            ffn_gain[0][:, None],
            jnp.pad(rel_table[0], ((0, piece - rel_table.shape[1]), (0, 0))),
            router_weight[0],
            jnp.zeros((piece, 128 - used), jnp.bfloat16),
        ],
        axis=1,
    )
    ids = jnp.pad(routes[0, :, :, 0].astype(jnp.bfloat16), ((0, 16 - micro_count), (0, 0)))
    attn_all, small_all, ids_all, in_all, out_all = collect_weights(
        attn, small, ids, expert_in[0, 0], expert_out[0, 0]
    )
    offset_ids = offset_buckets(length)
    offset_table = (offset_ids[:, None] == jnp.arange(BUCKETS, dtype=jnp.int32)[None, :]).astype(
        jnp.float32
    )
    labels = lax.dynamic_index_in_dim(segments, section, 0, keepdims=False)
    current = lax.dynamic_index_in_dim(inputs, section, 0, keepdims=False)
    layer_weights = []
    kept_list = []
    outputs = []
    for layer in range(layers):
        matrices = attn_all[layer]
        columns = small_all[layer]
        flat = columns.reshape(model_width, -1)
        weights = (
            flat[:, 0].astype(jnp.float32),
            jnp.concatenate(
                [matrices[:, which].reshape(model_width, -1) for which in range(3)], axis=1
            ),
            matrices[:, 3].reshape(model_width, -1),
            columns[:, : rel_table.shape[1], 2 : 2 + heads_here].reshape(BUCKETS, heads_here),
            flat[:, 1].astype(jnp.float32),
            flat[:, 2 + heads_here : used].astype(jnp.float32),
        )
        route_ids = lax.dynamic_index_in_dim(ids_all[layer], section, 0, keepdims=False).astype(
            jnp.int32
        )
        layer_weights.append((weights, route_ids))
        current, kept_state = forward_layer(
            current, weights, route_ids, labels, offset_table, in_all[layer], out_all[layer]
        )
        kept_list.append(kept_state)
        outputs.append(current)
    grad = lax.dynamic_index_in_dim(cotangent, section, 0, keepdims=False)
    input_grads = [None] * layers
    packs = [None] * layers
    for layer in reversed(range(layers)):
        weights, route_ids = layer_weights[layer]
        grad, attn_terms, expert_terms = backward_layer(
            grad,
            kept_list[layer],
            weights,
            route_ids,
            labels,
            offset_table,
            in_all[layer],
            out_all[layer],
        )
        input_grads[layer] = grad
        packs[layer] = pack_terms(attn_terms, expert_count) + expert_terms
    others = [
        jax.tree.map(
            lambda a: lax.ppermute(a.astype(jnp.bfloat16), "section", [(1 - layer, layer)]),
            packs[layer],
        )
        for layer in range(layers)
    ]
    summed = jax.tree.map(
        lambda a, b: a.astype(jnp.float32) + b.astype(jnp.float32), packs, others
    )
    grads, small_grads, grad_in, grad_out = jax.tree.map(
        lambda a, b: jnp.where(section == 0, a, b), *summed
    )
    grads, small_grads = reduce_grads(grads.astype(jnp.bfloat16), small_grads.astype(jnp.bfloat16))
    return (
        swap_micro(outputs),
        swap_micro(input_grads),
        small_grads[None, :, 0],
        grads[0][None],
        grads[1][None],
        grads[2][None],
        grads[3][None],
        small_grads[None, : rel_table.shape[1], 2 : 2 + heads_here],
        small_grads[None, :, 1],
        small_grads[None, :, 2 + heads_here : used],
        grad_in[None, None],
        grad_out[None, None],
    )


def solution(mesh):
    return jax.shard_map(
        local,
        mesh=mesh,
        in_specs=(
            P(None, "expert", None),
            P(None, "expert", None),
            P("section", "expert"),
            P("section", "expert", "tensor"),
            P("section", "expert", "tensor"),
            P("section", "expert", "tensor"),
            P("section", "expert", "tensor"),
            P("section", "expert", "tensor"),
            P("section", "expert"),
            P("section", "expert", None),
            P("section", "expert", None, "tensor"),
            P("section", "expert", "tensor", None),
            P("section", None, "expert", None),
            P(None, "expert"),
        ),
        out_specs=(
            P("section", None, "expert", None),
            P("section", None, "expert", None),
            P("section", "expert"),
            P("section", "expert", "tensor"),
            P("section", "expert", "tensor"),
            P("section", "expert", "tensor"),
            P("section", "expert", "tensor"),
            P("section", "expert", "tensor"),
            P("section", "expert"),
            P("section", "expert", None),
            P("section", "expert", None, "tensor"),
            P("section", "expert", "tensor", None),
        ),
        check_vma=False,
    )
```

```python
import math

import jax
import jax.numpy as jnp
from jax import lax
from jax.experimental import pallas as pl
from jax.experimental.pallas import tpu as pltpu
from jax.sharding import PartitionSpec as P

BUCKETS = 32


PEERS = 4
MESH = pl.DeviceIdType.MESH


def use_kernels():
    return (
        lax.axis_size("expert") == PEERS
        and lax.axis_size("tensor") == PEERS
        and lax.axis_size("section") == 2
    )


def around(axis, distance):
    return lax.rem(lax.axis_index(axis) + distance, PEERS)


def greet(axes, sibling=False):
    barrier = pltpu.get_barrier_semaphore()
    count = 0
    for axis in axes:
        for distance in range(1, PEERS):
            pl.semaphore_signal(
                barrier, inc=1, device_id={axis: around(axis, distance)}, device_id_type=MESH
            )
            count += 1
    if sibling:
        pl.semaphore_signal(
            barrier,
            inc=1,
            device_id={"section": 1 - lax.axis_index("section")},
            device_id_type=MESH,
        )
        count += 1
    pl.semaphore_wait(barrier, count)


def send(source, target, sends, receives, slot, axis, peer):
    copy = pltpu.make_async_remote_copy(
        src_ref=source,
        dst_ref=target,
        send_sem=sends.at[slot],
        recv_sem=receives.at[slot],
        device_id={axis: peer},
        device_id_type=MESH,
    )
    copy.start()
    return copy


def params(number):
    return pltpu.CompilerParams(
        collective_id=number, has_side_effects=True, vmem_limit_bytes=40 * 1024 * 1024
    )


def sems(count):
    return [pltpu.SemaphoreType.DMA((count,)), pltpu.SemaphoreType.DMA((count,))]


VMEM = pl.BlockSpec(memory_space=pltpu.VMEM)
ANY = pl.BlockSpec(memory_space=pl.ANY)


def start_kernel(
    attn, small, ids, first, second,
    attn_all, small_all, ids_all, first_all, second_all,
    near_send, near_recv, far_send, far_recv, pass_send, pass_recv, here,
):
    section = lax.axis_index("section")
    expert = lax.axis_index("expert")
    other = 1 - section
    greet(["expert"], sibling=True)
    far = []
    for distance in range(1, PEERS):
        peer = around("expert", distance)
        far.append([
            send(attn, attn_all.at[section, expert], far_send, far_recv, 2 * distance - 2, "expert", peer),
            send(small, small_all.at[section, expert], far_send, far_recv, 2 * distance - 1, "expert", peer),
        ])
    pairs = [
        (attn, attn_all.at[section, expert]),
        (small, small_all.at[section, expert]),
        (ids, ids_all.at[section]),
        (first, first_all.at[section]),
        (second, second_all.at[section]),
    ]
    near = []
    own = []
    for slot, (source, target) in enumerate(pairs):
        near.append(send(source, target, near_send, near_recv, slot, "section", other))
        copy = pltpu.make_async_copy(source, target, here.at[slot])
        copy.start()
        own.append(copy)
    passed = []
    for distance in range(1, PEERS):
        origin = around("expert", PEERS - distance)
        for copy in far[distance - 1]:
            copy.wait_recv()
        for which, whole in enumerate((attn_all, small_all)):
            place = whole.at[section, origin]
            passed.append(
                send(place, place, pass_send, pass_recv, 2 * distance - 2 + which, "section", other)
            )
    for copy in own:
        copy.wait()
    for copy in near + passed:
        copy.wait()
    for group in far:
        for copy in group:
            copy.wait_send()


def collect_weights(attn, small, ids, first, second):
    if not use_kernels():
        over = lambda a: lax.all_gather(a, "section")
        return (
            over(lax.all_gather(attn, "expert")),
            over(lax.all_gather(small, "expert")),
            over(ids),
            over(first),
            over(second),
        )
    shapes = [
        (2, PEERS) + attn.shape,
        (2, PEERS) + small.shape,
        (2,) + ids.shape,
        (2,) + first.shape,
        (2,) + second.shape,
    ]
    return pl.pallas_call(
        start_kernel,
        out_shape=[jax.ShapeDtypeStruct(shape, jnp.bfloat16) for shape in shapes],
        in_specs=[ANY] * 5,
        out_specs=[ANY] * 5,
        scratch_shapes=sems(5) + sems(6) + sems(6) + [pltpu.SemaphoreType.DMA((5,))],
        compiler_params=params(1),
    )(attn, small, ids, first, second)


def total_kernel(part, whole, landed, send_one, recv_one, send_two, recv_two):
    own = lax.axis_index("tensor")
    greet(["tensor"])
    one = []
    for distance in range(1, PEERS):
        peer = around("tensor", distance)
        one.append(
            send(part.at[peer], landed.at[distance - 1], send_one, recv_one, distance - 1, "tensor", peer)
        )
    total = part[own].astype(jnp.float32)
    for slot, copy in enumerate(one):
        copy.wait_recv()
        total = total + landed[slot].astype(jnp.float32)
    whole[own] = total.astype(whole.dtype)
    two = []
    for distance in range(1, PEERS):
        peer = around("tensor", distance)
        two.append(
            send(whole.at[own], whole.at[own], send_two, recv_two, distance - 1, "tensor", peer)
        )
    for copy in two:
        copy.wait()
    for copy in one:
        copy.wait_send()


def sum_heads(part):
    if not use_kernels():
        return lax.psum(part, "tensor")
    length, width = part.shape
    split = part.reshape(PEERS, length // PEERS, width)
    return pl.pallas_call(
        total_kernel,
        out_shape=jax.ShapeDtypeStruct(split.shape, split.dtype),
        in_specs=[VMEM],
        out_specs=VMEM,
        scratch_shapes=[pltpu.VMEM((PEERS - 1,) + split.shape[1:], split.dtype)] + sems(3) + sems(3),
        compiler_params=params(2),
    )(split).reshape(length, width)


def joined(parts):
    count, groups, capacity, width = parts.shape
    return jnp.concatenate(
        [parts[index].reshape(groups * capacity, width) for index in range(count)], axis=-1
    )


def share_rows(own_rows, pick, rows, whole, first, second):
    own = lax.axis_index("tensor")
    expert = lax.axis_index("expert")
    rows[...] = (
        lax.dot_general(
            pick[...], own_rows[...], (((0,), (0,)), ((), ())), preferred_element_type=jnp.float32
        )
        .astype(rows.dtype)
        .reshape(rows.shape)
    )
    greet(["tensor", "expert"])
    one = []
    for distance in range(1, PEERS):
        peer = around("expert", distance)
        one.append(send(rows.at[peer], whole.at[own, expert], *first, distance - 1, "expert", peer))
    whole[own, expert] = rows[expert]
    for copy in one:
        copy.wait_recv()
    two = []
    for distance in range(1, PEERS):
        peer = around("tensor", distance)
        two.append(send(whole.at[own], whole.at[own], *second, distance - 1, "tensor", peer))
    for copy in two:
        copy.wait_recv()
    return one + two


def return_rows(values, pick, part, landed, reduced, arrived, back, out, first, second, third, beside):
    own = lax.axis_index("tensor")
    expert = lax.axis_index("expert")
    width = part.shape[3]
    for index in range(PEERS):
        part[index] = (
            values[:, index * width : (index + 1) * width].astype(part.dtype).reshape(part.shape[1:])
        )
    one = []
    for distance in range(1, PEERS):
        peer = around("tensor", distance)
        one.append(send(part.at[peer], landed.at[distance - 1], *first, distance - 1, "tensor", peer))
    if beside is not None:
        beside()
    for copy in one:
        copy.wait_recv()
    total = part[own].astype(jnp.float32)
    for slot in range(PEERS - 1):
        total = total + landed[slot].astype(jnp.float32)
    reduced[...] = total.astype(reduced.dtype)
    two = []
    for distance in range(1, PEERS):
        peer = around("expert", distance)
        two.append(send(reduced.at[peer], arrived.at[expert], *second, distance - 1, "expert", peer))
    arrived[expert] = reduced[expert]
    for copy in two:
        copy.wait_recv()
    groups, capacity, width = arrived.shape
    back[own] = jnp.dot(
        pick[...],
        arrived[...].reshape(groups * capacity, width),
        preferred_element_type=jnp.float32,
    ).astype(back.dtype)
    three = []
    for distance in range(1, PEERS):
        peer = around("tensor", distance)
        three.append(send(back.at[own], back.at[own], *third, distance - 1, "tensor", peer))
    for copy in three:
        copy.wait_recv()
    out[...] = jnp.concatenate([back[index] for index in range(PEERS)], axis=-1)
    return one + two + three


def expert_kernel(
    own_rows, pick, weight_in, weight_out,
    out, groups, hidden_out, active_out,
    rows, landed, part, reduced, arrived, back, whole, *pairs,
):
    pairs = [pairs[2 * index : 2 * index + 2] for index in range(5)]
    copies = share_rows(own_rows, pick, rows, whole, pairs[0], pairs[1])
    together = joined(whole)
    groups[...] = together
    hidden = jnp.dot(together, weight_in[...], preferred_element_type=jnp.float32)
    active = jax.nn.gelu(hidden).astype(jnp.bfloat16)
    values = jnp.dot(active, weight_out[...], preferred_element_type=jnp.float32)

    def keep():
        hidden_out[...] = hidden
        active_out[...] = active

    copies += return_rows(
        values, pick, part, landed, reduced, arrived, back, out, pairs[2], pairs[3], pairs[4], keep
    )
    for copy in copies:
        copy.wait_send()


def gelu_slope(values):
    scale = (2.0 / math.pi) ** 0.5
    square = values * values
    bent = jnp.tanh(scale * values * (1.0 + 0.044715 * square))
    return 0.5 * (1.0 + bent) + 0.5 * values * (1.0 - bent * bent) * scale * (
        1.0 + 3 * 0.044715 * square
    )


def expert_back_kernel(
    own_rows, pick, weight_in, weight_out, groups, hidden, active,
    out, grad_in, grad_out,
    rows, landed, part, reduced, arrived, back, whole, *pairs,
):
    pairs = [pairs[2 * index : 2 * index + 2] for index in range(5)]
    copies = share_rows(own_rows, pick, rows, whole, pairs[0], pairs[1])
    together = joined(whole)
    grad_active = lax.dot_general(
        together, weight_out[...], (((1,), (1,)), ((), ())), preferred_element_type=jnp.float32
    )
    grad_hidden = (grad_active * gelu_slope(hidden[...])).astype(jnp.bfloat16)
    values = lax.dot_general(
        grad_hidden, weight_in[...], (((1,), (1,)), ((), ())), preferred_element_type=jnp.float32
    )

    def weights():
        grad_in[...] = lax.dot_general(
            groups[...], grad_hidden, (((0,), (0,)), ((), ())), preferred_element_type=jnp.float32
        ).astype(grad_in.dtype)
        grad_out[...] = lax.dot_general(
            active[...], together, (((0,), (0,)), ((), ())), preferred_element_type=jnp.float32
        ).astype(grad_out.dtype)

    copies += return_rows(
        values, pick, part, landed, reduced, arrived, back, out, pairs[2], pairs[3], pairs[4], weights
    )
    for copy in copies:
        copy.wait_send()


def expert_call(kernel, number, outs, experts, capacity, operands):
    length, width = operands[0].shape
    low = jnp.bfloat16
    block = (experts, capacity, width)
    return pl.pallas_call(
        kernel,
        out_shape=outs,
        in_specs=[VMEM] * len(operands),
        out_specs=[VMEM] * len(outs),
        scratch_shapes=[
            pltpu.VMEM(block, low),
            pltpu.VMEM((PEERS - 1,) + block, low),
            pltpu.VMEM((PEERS,) + block, low),
            pltpu.VMEM(block, low),
            pltpu.VMEM(block, low),
            pltpu.VMEM((PEERS, length, width), low),
            pltpu.VMEM((PEERS,) + block, low),
        ]
        + sems(3) * 5,
        compiler_params=params(number),
    )(*operands)


def to_experts(own_rows, pick, experts, capacity):
    rows = lax.dot_general(
        pick, own_rows, (((0,), (0,)), ((), ())), preferred_element_type=jnp.float32
    ).astype(jnp.bfloat16)
    arrived = lax.all_to_all(
        rows.reshape(experts, capacity, -1), "expert", split_axis=0, concat_axis=0, tiled=True
    )
    return lax.all_gather(arrived.reshape(experts * capacity, -1), "tensor", axis=1, tiled=True)


def from_experts(values, pick, experts, capacity):
    share = lax.psum_scatter(
        values.astype(jnp.bfloat16), "tensor", scatter_dimension=1, tiled=True
    )
    returned = lax.all_to_all(
        share.reshape(experts, capacity, -1), "expert", split_axis=0, concat_axis=0, tiled=True
    )
    picked = jnp.dot(
        pick, returned.reshape(experts * capacity, -1), preferred_element_type=jnp.float32
    ).astype(jnp.bfloat16)
    return lax.all_gather(picked, "tensor", axis=1, tiled=True)


def run_experts(own_rows, pick, weight_in, weight_out, experts, capacity):
    if use_kernels():
        length = own_rows.shape[0]
        width, hidden_width = weight_in.shape
        slots = experts * capacity
        return expert_call(
            expert_kernel,
            3,
            [
                jax.ShapeDtypeStruct((length, width), jnp.bfloat16),
                jax.ShapeDtypeStruct((slots, width), jnp.bfloat16),
                jax.ShapeDtypeStruct((slots, hidden_width), jnp.float32),
                jax.ShapeDtypeStruct((slots, hidden_width), jnp.bfloat16),
            ],
            experts,
            capacity,
            (own_rows, pick, weight_in, weight_out),
        )
    groups = to_experts(own_rows, pick, experts, capacity)
    hidden = jnp.dot(groups, weight_in, preferred_element_type=jnp.float32)
    active = jax.nn.gelu(hidden).astype(jnp.bfloat16)
    values = jnp.dot(active, weight_out, preferred_element_type=jnp.float32)
    return (from_experts(values, pick, experts, capacity), groups, hidden, active)


def run_experts_back(
    own_rows, pick, weight_in, weight_out, groups, hidden, active, experts, capacity
):
    if use_kernels():
        return expert_call(
            expert_back_kernel,
            4,
            [
                jax.ShapeDtypeStruct((own_rows.shape[0], weight_in.shape[0]), jnp.bfloat16),
                jax.ShapeDtypeStruct(weight_in.shape, jnp.bfloat16),
                jax.ShapeDtypeStruct(weight_out.shape, jnp.bfloat16),
            ],
            experts,
            capacity,
            (own_rows, pick, weight_in, weight_out, groups, hidden, active),
        )
    grad_groups = to_experts(own_rows, pick, experts, capacity)
    grad_active = lax.dot_general(
        grad_groups, weight_out, (((1,), (1,)), ((), ())), preferred_element_type=jnp.float32
    )
    grad_hidden = (grad_active * gelu_slope(hidden)).astype(jnp.bfloat16)
    values = lax.dot_general(
        grad_hidden, weight_in, (((1,), (1,)), ((), ())), preferred_element_type=jnp.float32
    )
    grad_in = lax.dot_general(
        groups, grad_hidden, (((0,), (0,)), ((), ())), preferred_element_type=jnp.float32
    ).astype(jnp.bfloat16)
    grad_out = lax.dot_general(
        active, grad_groups, (((0,), (0,)), ((), ())), preferred_element_type=jnp.float32
    ).astype(jnp.bfloat16)
    return (from_experts(values, pick, experts, capacity), grad_in, grad_out)


def finish_kernel(
    normed, joint, attn, mixed, small, grads_out, small_out,
    give, give_small, came, came_small, summed, summed_small, landed, landed_small,
    near_send, near_recv, far_send, far_recv,
):
    section = lax.axis_index("section")
    expert = lax.axis_index("expert")
    other = 1 - section
    piece = summed.shape[1:3]
    columns = mixed.shape[2]

    def product(layer, index):
        pair = (normed[layer], joint[layer, index]) if index < 3 else (attn[layer], mixed[layer])
        whole = lax.dot_general(
            *pair, (((0,), (0,)), ((), ())), preferred_element_type=jnp.float32
        )
        return whole.reshape((PEERS, whole.shape[0] // PEERS, columns))

    for index in range(4):
        give[index] = product(other, index).astype(give.dtype)
    give_small[...] = small[other].astype(give_small.dtype)
    greet(["expert"], sibling=True)
    near = []
    for index in range(4):
        near.append(send(give.at[index], came.at[index], near_send, near_recv, index, "section", other))
    near.append(send(give_small, came_small, near_send, near_recv, 4, "section", other))
    copies = []
    near[4].wait_recv()
    summed_small[...] = (small[section] + came_small[...].astype(jnp.float32)).astype(summed_small.dtype)
    for distance in range(1, PEERS):
        peer = around("expert", distance)
        slot = distance - 1
        copies.append(
            (4, slot, send(summed_small.at[peer], landed_small.at[slot], far_send, far_recv, 12 + slot, "expert", peer))
        )
    for index in range(4):
        mine = product(section, index)
        near[index].wait_recv()
        summed[index] = (mine + came[index].astype(jnp.float32)).astype(summed.dtype)
        for distance in range(1, PEERS):
            peer = around("expert", distance)
            slot = distance - 1
            copies.append(
                (index, slot, send(summed.at[index, peer], landed.at[index, slot], far_send, far_recv, 3 * index + slot, "expert", peer))
            )
    small_out[...] = summed_small[expert].astype(jnp.float32)
    for index in range(4):
        grads_out[index] = summed[index, expert].astype(jnp.float32)
    for index, slot, copy in copies:
        copy.wait_recv()
        if index == 4:
            small_out[...] += landed_small[slot].astype(jnp.float32)
        else:
            grads_out[index] += landed[index, slot].astype(jnp.float32)
    for copy in near:
        copy.wait_send()
    for index, slot, copy in copies:
        copy.wait_send()


def reduce_grads(normed, joint, attn, mixed, small):
    experts = lax.axis_size("expert")
    layers, length, width = normed.shape
    piece = width // experts
    columns = mixed.shape[2]
    low = jnp.bfloat16
    if not use_kernels():
        section = lax.axis_index("section")
        outer = lambda a, b: jnp.einsum(
            "lta,ltb->lab", a, b, preferred_element_type=jnp.float32
        ).reshape(layers, experts, piece, columns)
        grads = jnp.stack(
            [outer(normed, joint[:, index]) for index in range(3)] + [outer(attn, mixed)], axis=2
        )
        results = []
        for part in (grads, small):
            scattered = lax.psum_scatter(
                part.astype(low), "expert", scatter_dimension=1, tiled=False
            ).astype(jnp.float32)
            own = lax.dynamic_index_in_dim(scattered, section, 0, keepdims=False)
            far = lax.dynamic_index_in_dim(scattered, 1 - section, 0, keepdims=False).astype(low)
            came = lax.ppermute(far, "section", [(0, 1), (1, 0)])
            results.append(own + came.astype(jnp.float32))
        return results
    return pl.pallas_call(
        finish_kernel,
        out_shape=[
            jax.ShapeDtypeStruct((4, piece, columns), jnp.float32),
            jax.ShapeDtypeStruct((piece, 128), jnp.float32),
        ],
        in_specs=[VMEM] * 5,
        out_specs=[VMEM] * 2,
        scratch_shapes=[
            pltpu.VMEM((4, PEERS, piece, columns), low),
            pltpu.VMEM((PEERS, piece, 128), low),
            pltpu.VMEM((4, PEERS, piece, columns), low),
            pltpu.VMEM((PEERS, piece, 128), low),
            pltpu.VMEM((4, PEERS, piece, columns), low),
            pltpu.VMEM((PEERS, piece, 128), low),
            pltpu.VMEM((4, PEERS - 1, piece, columns), low),
            pltpu.VMEM((PEERS - 1, piece, 128), low),
        ]
        + sems(5)
        + sems(15),
        compiler_params=params(5),
    )(normed, joint, attn, mixed, small)


def own_features(rows):
    width = rows.shape[1] // lax.axis_size("tensor")
    return lax.dynamic_slice_in_dim(rows, lax.axis_index("tensor") * width, width, 1)


def slots_for(length, experts):
    capacity = 5 * length // (4 * experts)
    return -(-capacity // 16) * 16


def offset_buckets(length):
    half_count = BUCKETS // 2
    exact_count = half_count // 2
    offsets = jnp.arange(2 * length, dtype=jnp.int32) - (length - 1)
    distance = jnp.abs(offsets)
    larger = jnp.full_like(distance, exact_count)
    for level_index in range(1, half_count - exact_count):
        border = int(
            math.ceil(
                exact_count * (128.0 / exact_count) ** (level_index / (half_count - exact_count))
                - 1e-09
            )
        )
        larger = larger + (distance >= border).astype(jnp.int32)
    bucket = jnp.where(distance < exact_count, distance, larger)
    return bucket + jnp.where(offsets > 0, half_count, 0)


def spread_offsets(per_offset, length):
    heads_here = per_offset.shape[0]
    tiled = jnp.tile(per_offset, (1, length))[:, : length * (2 * length - 1)]
    skewed = tiled.reshape(heads_here, length, 2 * length - 1)
    return skewed[:, :, length - 1 :]


def collect_offsets(grid_values, length):
    heads_here = grid_values.shape[0]
    padded = jnp.pad(grid_values, ((0, 0), (0, 0), (length - 1, 0)))
    flat = jnp.pad(padded.reshape(heads_here, length * (2 * length - 1)), ((0, 0), (0, length)))
    return jnp.sum(flat.reshape(heads_here, length, 2 * length), axis=1, dtype=jnp.float32)


def rms_scale(values, gain_vector):
    return (
        values * lax.rsqrt(jnp.mean(values * values, axis=-1, keepdims=True) + 1e-06) * gain_vector
    )


def slot_places(route_ids, experts, capacity):
    chosen = route_ids[:, None] == jnp.arange(experts, dtype=jnp.int32)[None, :]
    counts = jnp.cumsum(chosen.astype(jnp.int32), axis=0)
    slot_number = jnp.sum(jnp.where(chosen, counts, 0), axis=-1) - 1
    return (chosen, route_ids * capacity + slot_number)


def position_bias(offset_table, bias_table, length):
    per_offset = jnp.dot(
        offset_table, bias_table.astype(jnp.float32), precision=lax.Precision.HIGHEST
    )
    return spread_offsets(per_offset.T, length)


def attention_probs(query_heads, key_heads, rel_bias, labels, head_size):
    scores = (
        jnp.einsum("qhe,khe->hqk", query_heads, key_heads, preferred_element_type=jnp.float32)
        * head_size ** (-0.5)
        + rel_bias
    )
    same_doc = labels[:, None] == labels[None, :]
    return jnp.where(same_doc[None], scores, -1000000000.0)


def forward_layer(layer_in, weights, route_ids, labels, offset_table, weight_in, weight_out):
    gain_one, joint_weight, attn_out_weight, bias_table, gain_two, router_matrix = weights
    length, model_width = layer_in.shape
    heads_here = bias_table.shape[1]
    head_size = attn_out_weight.shape[1] // heads_here
    experts = router_matrix.shape[1]
    capacity = slots_for(length, experts)
    input_float = layer_in.astype(jnp.float32)
    normed = rms_scale(input_float, gain_one).astype(jnp.bfloat16)
    joint_heads = jnp.dot(normed, joint_weight, preferred_element_type=jnp.float32).astype(
        jnp.bfloat16
    )
    query_heads, key_heads, value_heads = [
        part.reshape(length, heads_here, head_size) for part in jnp.split(joint_heads, 3, axis=1)
    ]
    rel_bias = position_bias(offset_table, bias_table, length)
    scores = attention_probs(query_heads, key_heads, rel_bias, labels, head_size)
    log_total = jax.nn.logsumexp(scores, axis=-1)
    probs_low = jnp.exp(scores - log_total[..., None]).astype(jnp.bfloat16)
    mixed_heads = (
        jnp.einsum("hqk,khe->qhe", probs_low, value_heads, preferred_element_type=jnp.float32)
        .astype(jnp.bfloat16)
        .reshape(length, heads_here * head_size)
    )
    partial_out = lax.dot_general(
        mixed_heads, attn_out_weight, (((1,), (1,)), ((), ())), preferred_element_type=jnp.float32
    )
    residual = input_float + sum_heads(partial_out.astype(jnp.bfloat16)).astype(jnp.float32)
    normed_two = rms_scale(residual, gain_two)
    logits = jnp.dot(normed_two, router_matrix, precision=lax.Precision.HIGHEST)
    router_probs = jax.nn.softmax(logits, axis=-1)
    chosen, slot_index = slot_places(route_ids, experts, capacity)
    gate_value = jnp.sum(jnp.where(chosen, router_probs, 0.0), axis=-1, keepdims=True)
    pick = (
        slot_index[:, None] == jnp.arange(experts * capacity, dtype=jnp.int32)[None, :]
    ).astype(jnp.bfloat16)
    expert_low, groups, hidden, active = run_experts(
        own_features(normed_two).astype(jnp.bfloat16),
        pick,
        weight_in,
        weight_out,
        experts,
        capacity,
    )
    output = (residual + gate_value * expert_low.astype(jnp.float32)).astype(jnp.bfloat16)
    kept_state = (
        layer_in,
        normed,
        query_heads,
        key_heads,
        value_heads,
        mixed_heads,
        log_total,
        residual,
        router_probs,
        gate_value,
        pick,
        groups,
        hidden,
        active,
        expert_low,
    )
    return (output, kept_state)


def backward_layer(
    grad_out, kept_state, weights, route_ids, labels, offset_table, weight_in, weight_out
):
    (
        layer_in,
        normed,
        query_heads,
        key_heads,
        value_heads,
        mixed_heads,
        log_total,
        residual,
        router_probs,
        gate_value,
        pick,
        groups,
        hidden,
        active,
        expert_low,
    ) = kept_state
    gain_one, joint_weight, attn_out_weight, bias_table, gain_two, router_matrix = weights
    length, model_width = layer_in.shape
    heads_here = bias_table.shape[1]
    head_size = attn_out_weight.shape[1] // heads_here
    experts = router_matrix.shape[1]
    capacity = slots_for(length, experts)
    grad_float = grad_out.astype(jnp.float32)
    grad_gate = jnp.sum(grad_float * expert_low.astype(jnp.float32), axis=-1, keepdims=True)
    grad_value = (gate_value * grad_float).astype(jnp.bfloat16)
    grad_rows, grad_weight_in, grad_weight_out = run_experts_back(
        own_features(grad_value),
        pick,
        weight_in,
        weight_out,
        groups,
        hidden,
        active,
        experts,
        capacity,
    )
    grad_normed_two = grad_rows.astype(jnp.float32)
    chosen = route_ids[:, None] == jnp.arange(experts, dtype=jnp.int32)[None, :]
    grad_logits = grad_gate * gate_value * (chosen.astype(jnp.float32) - router_probs)
    grad_normed_two = grad_normed_two + lax.dot_general(
        grad_logits, router_matrix, (((1,), (1,)), ((), ())), precision=lax.Precision.HIGHEST
    )
    normed_two, norm_pull = jax.vjp(rms_scale, residual, gain_two)
    grad_router = lax.dot_general(
        normed_two, grad_logits, (((0,), (0,)), ((), ())), precision=lax.Precision.HIGHEST
    )
    grad_residual, grad_gain_two = norm_pull(grad_normed_two)
    grad_residual = grad_residual + grad_float
    grad_attn = grad_residual.astype(jnp.bfloat16)
    grad_mixed = (
        jnp.dot(grad_attn, attn_out_weight, preferred_element_type=jnp.float32)
        .astype(jnp.bfloat16)
        .reshape(length, heads_here, head_size)
    )
    rel_bias = position_bias(offset_table, bias_table, length)
    scores = attention_probs(query_heads, key_heads, rel_bias, labels, head_size)
    probs_float = jnp.exp(scores - log_total[..., None])
    probs_low = probs_float.astype(jnp.bfloat16)
    grad_probs = jnp.einsum(
        "qhe,khe->hqk", grad_mixed, value_heads, preferred_element_type=jnp.float32
    )
    grad_scores = (
        probs_float * (grad_probs - jnp.sum(probs_float * grad_probs, axis=-1, keepdims=True))
    ).astype(jnp.bfloat16)
    grad_query = (
        jnp.einsum("hqk,khe->qhe", grad_scores, key_heads, preferred_element_type=jnp.float32)
        * head_size ** (-0.5)
    ).astype(jnp.bfloat16)
    grad_keys = (
        jnp.einsum("hqk,qhe->khe", grad_scores, query_heads, preferred_element_type=jnp.float32)
        * head_size ** (-0.5)
    ).astype(jnp.bfloat16)
    grad_values = jnp.einsum(
        "hqk,qhe->khe", probs_low, grad_mixed, preferred_element_type=jnp.float32
    ).astype(jnp.bfloat16)
    offset_sums = collect_offsets(grad_scores, length)
    grad_table = jnp.einsum("kb,hk->bh", offset_table, offset_sums, precision=lax.Precision.HIGHEST)
    grad_joint = jnp.concatenate(
        [
            part.reshape(length, heads_here * head_size)
            for part in (grad_query, grad_keys, grad_values)
        ],
        axis=1,
    )
    grad_normed_part = lax.dot_general(
        grad_joint, joint_weight, (((1,), (1,)), ((), ())), preferred_element_type=jnp.float32
    )
    grad_normed = sum_heads(grad_normed_part.astype(jnp.bfloat16)).astype(jnp.float32)
    input_pull = jax.vjp(rms_scale, layer_in.astype(jnp.float32), gain_one)[1]
    grad_input_part, grad_gain_one = input_pull(grad_normed)
    grad_input = (grad_residual + grad_input_part).astype(jnp.bfloat16)
    small_terms = (grad_gain_one, grad_table, grad_gain_two, grad_router)
    joint_terms = jnp.stack(
        [
            part.reshape(length, heads_here * head_size)
            for part in (grad_query, grad_keys, grad_values)
        ]
    )
    return (
        grad_input,
        small_terms,
        (normed, joint_terms, grad_attn, mixed_heads),
        (grad_weight_in, grad_weight_out),
    )


def pack_terms(small_terms, expert_count):
    gain_one, table, gain_two, router = small_terms
    width = gain_one.shape[0]
    piece = width // expert_count
    rows = table.shape[0] // expert_count
    table = jnp.pad(
        table.reshape(expert_count, rows, -1), ((0, 0), (0, piece - rows), (0, 0))
    ).reshape(width, -1)
    used = 2 + table.shape[1] + router.shape[1]
    return jnp.concatenate(
        [
            gain_one[:, None],
            gain_two[:, None],
            table,
            router,
            jnp.zeros((width, 128 - used), jnp.float32),
        ],
        axis=1,
    ).reshape(expert_count, piece, 128)


def swap_micro(per_layer):
    section = lax.axis_index("section")
    own = jnp.where(section == 0, per_layer[0], per_layer[1])
    other = jnp.where(section == 0, per_layer[1], per_layer[0])
    came = lax.ppermute(other, "section", [(0, 1), (1, 0)])
    return jnp.where(
        section == 0, jnp.stack([own, came]), jnp.stack([came, own])
    )[None]


def local(
    inputs,
    cotangent,
    attn_gain,
    query_weight,
    key_weight,
    value_weight,
    out_weight,
    rel_table,
    ffn_gain,
    router_weight,
    expert_in,
    expert_out,
    routes,
    segments,
):
    section = lax.axis_index("section")
    layers = lax.axis_size("section")
    expert_count = lax.axis_size("expert")
    micro_count, length, model_width = inputs.shape
    heads_here = rel_table.shape[2]
    experts = router_weight.shape[2]
    piece = attn_gain.shape[1]
    attn = jnp.concatenate([query_weight, key_weight, value_weight, out_weight], axis=0)
    used = 2 + heads_here + experts
    small = jnp.concatenate(
        [
            attn_gain[0][:, None],
            ffn_gain[0][:, None],
            jnp.pad(rel_table[0], ((0, piece - rel_table.shape[1]), (0, 0))),
            router_weight[0],
            jnp.zeros((piece, 128 - used), jnp.bfloat16),
        ],
        axis=1,
    )
    ids = jnp.pad(routes[0, :, :, 0].astype(jnp.bfloat16), ((0, 16 - micro_count), (0, 0)))
    attn_all, small_all, ids_all, in_all, out_all = collect_weights(
        attn, small, ids, expert_in[0, 0], expert_out[0, 0]
    )
    offset_ids = offset_buckets(length)
    offset_table = (offset_ids[:, None] == jnp.arange(BUCKETS, dtype=jnp.int32)[None, :]).astype(
        jnp.float32
    )
    labels = lax.dynamic_index_in_dim(segments, section, 0, keepdims=False)
    current = lax.dynamic_index_in_dim(inputs, section, 0, keepdims=False)
    layer_weights = []
    kept_list = []
    outputs = []
    for layer in range(layers):
        matrices = attn_all[layer]
        columns = small_all[layer]
        flat = columns.reshape(model_width, -1)
        weights = (
            flat[:, 0].astype(jnp.float32),
            jnp.concatenate(
                [matrices[:, which].reshape(model_width, -1) for which in range(3)], axis=1
            ),
            matrices[:, 3].reshape(model_width, -1),
            columns[:, : rel_table.shape[1], 2 : 2 + heads_here].reshape(BUCKETS, heads_here),
            flat[:, 1].astype(jnp.float32),
            flat[:, 2 + heads_here : used].astype(jnp.float32),
        )
        route_ids = lax.dynamic_index_in_dim(ids_all[layer], section, 0, keepdims=False).astype(
            jnp.int32
        )
        layer_weights.append((weights, route_ids))
        current, kept_state = forward_layer(
            current, weights, route_ids, labels, offset_table, in_all[layer], out_all[layer]
        )
        kept_list.append(kept_state)
        outputs.append(current)
    grad = lax.dynamic_index_in_dim(cotangent, section, 0, keepdims=False)
    input_grads = [None] * layers
    packs = [None] * layers
    expert_packs = [None] * layers
    for layer in reversed(range(layers)):
        weights, route_ids = layer_weights[layer]
        grad, small_terms, wide_terms, expert_terms = backward_layer(
            grad,
            kept_list[layer],
            weights,
            route_ids,
            labels,
            offset_table,
            in_all[layer],
            out_all[layer],
        )
        input_grads[layer] = grad
        packs[layer] = wide_terms + (pack_terms(small_terms, expert_count),)
        expert_packs[layer] = expert_terms
    came = [
        jax.tree.map(
            lambda a: lax.ppermute(a, "section", [(1 - layer, layer)]), expert_packs[layer]
        )
        for layer in range(layers)
    ]
    grads, small_grads = reduce_grads(*[jnp.stack(pair) for pair in zip(*packs)])
    grad_in, grad_out = [
        jnp.where(section == 0, expert_packs[0][index], expert_packs[1][index]).astype(jnp.float32)
        + jnp.where(section == 0, came[0][index], came[1][index]).astype(jnp.float32)
        for index in range(2)
    ]
    return (
        swap_micro(outputs),
        swap_micro(input_grads),
        small_grads[None, :, 0],
        grads[0][None],
        grads[1][None],
        grads[2][None],
        grads[3][None],
        small_grads[None, : rel_table.shape[1], 2 : 2 + heads_here],
        small_grads[None, :, 1],
        small_grads[None, :, 2 + heads_here : used],
        grad_in[None, None],
        grad_out[None, None],
    )


def solution(mesh):
    return jax.shard_map(
        local,
        mesh=mesh,
        in_specs=(
            P(None, "expert", None),
            P(None, "expert", None),
            P("section", "expert"),
            P("section", "expert", "tensor"),
            P("section", "expert", "tensor"),
            P("section", "expert", "tensor"),
            P("section", "expert", "tensor"),
            P("section", "expert", "tensor"),
            P("section", "expert"),
            P("section", "expert", None),
            P("section", "expert", None, "tensor"),
            P("section", "expert", "tensor", None),
            P("section", None, "expert", None),
            P(None, "expert"),
        ),
        out_specs=(
            P("section", None, "expert", None),
            P("section", None, "expert", None),
            P("section", "expert"),
            P("section", "expert", "tensor"),
            P("section", "expert", "tensor"),
            P("section", "expert", "tensor"),
            P("section", "expert", "tensor"),
            P("section", "expert", "tensor"),
            P("section", "expert"),
            P("section", "expert", None),
            P("section", "expert", None, "tensor"),
            P("section", "expert", "tensor", None),
        ),
        check_vma=False,
    )
```

```python
import math

import jax
import jax.numpy as jnp
from jax import lax
from jax.experimental import pallas as pl
from jax.experimental.pallas import tpu as pltpu
from jax.sharding import PartitionSpec as P

BUCKETS = 32


PEERS = 4
MESH = pl.DeviceIdType.MESH


def use_kernels():
    return (
        lax.axis_size("expert") == PEERS
        and lax.axis_size("tensor") == PEERS
        and lax.axis_size("section") == 2
    )


def around(axis, distance):
    return lax.rem(lax.axis_index(axis) + distance, PEERS)


def greet(axes, sibling=False):
    barrier = pltpu.get_barrier_semaphore()
    count = 0
    for axis in axes:
        for distance in range(1, PEERS):
            pl.semaphore_signal(
                barrier, inc=1, device_id={axis: around(axis, distance)}, device_id_type=MESH
            )
            count += 1
    if sibling:
        pl.semaphore_signal(
            barrier,
            inc=1,
            device_id={"section": 1 - lax.axis_index("section")},
            device_id_type=MESH,
        )
        count += 1
    pl.semaphore_wait(barrier, count)


def send(source, target, sends, receives, slot, axis, peer):
    copy = pltpu.make_async_remote_copy(
        src_ref=source,
        dst_ref=target,
        send_sem=sends.at[slot],
        recv_sem=receives.at[slot],
        device_id={axis: peer},
        device_id_type=MESH,
    )
    copy.start()
    return copy


def params(number):
    return pltpu.CompilerParams(
        collective_id=number, has_side_effects=True, vmem_limit_bytes=40 * 1024 * 1024
    )


def sems(count):
    return [pltpu.SemaphoreType.DMA((count,)), pltpu.SemaphoreType.DMA((count,))]


VMEM = pl.BlockSpec(memory_space=pltpu.VMEM)
ANY = pl.BlockSpec(memory_space=pl.ANY)


def start_kernel(
    attn, small, ids, first, second,
    attn_all, small_all, ids_all, first_all, second_all,
    near_send, near_recv, far_send, far_recv, pass_send, pass_recv, here,
):
    section = lax.axis_index("section")
    expert = lax.axis_index("expert")
    other = 1 - section
    greet(["expert"], sibling=True)
    far = []
    for distance in range(1, PEERS):
        peer = around("expert", distance)
        far.append([
            send(attn, attn_all.at[section, expert], far_send, far_recv, 2 * distance - 2, "expert", peer),
            send(small, small_all.at[section, expert], far_send, far_recv, 2 * distance - 1, "expert", peer),
        ])
    pairs = [
        (attn, attn_all.at[section, expert]),
        (small, small_all.at[section, expert]),
        (ids, ids_all.at[section]),
        (first, first_all.at[section]),
        (second, second_all.at[section]),
    ]
    near = []
    own = []
    for slot, (source, target) in enumerate(pairs):
        near.append(send(source, target, near_send, near_recv, slot, "section", other))
        copy = pltpu.make_async_copy(source, target, here.at[slot])
        copy.start()
        own.append(copy)
    passed = []
    for distance in range(1, PEERS):
        origin = around("expert", PEERS - distance)
        for copy in far[distance - 1]:
            copy.wait_recv()
        for which, whole in enumerate((attn_all, small_all)):
            place = whole.at[section, origin]
            passed.append(
                send(place, place, pass_send, pass_recv, 2 * distance - 2 + which, "section", other)
            )
    for copy in own:
        copy.wait()
    for copy in near + passed:
        copy.wait()
    for group in far:
        for copy in group:
            copy.wait_send()


def collect_weights(attn, small, ids, first, second):
    if not use_kernels():
        over = lambda a: lax.all_gather(a, "section")
        return (
            over(lax.all_gather(attn, "expert")),
            over(lax.all_gather(small, "expert")),
            over(ids),
            over(first),
            over(second),
        )
    shapes = [
        (2, PEERS) + attn.shape,
        (2, PEERS) + small.shape,
        (2,) + ids.shape,
        (2,) + first.shape,
        (2,) + second.shape,
    ]
    return pl.pallas_call(
        start_kernel,
        out_shape=[jax.ShapeDtypeStruct(shape, jnp.bfloat16) for shape in shapes],
        in_specs=[ANY] * 5,
        out_specs=[ANY] * 5,
        scratch_shapes=sems(5) + sems(6) + sems(6) + [pltpu.SemaphoreType.DMA((5,))],
        compiler_params=params(1),
    )(attn, small, ids, first, second)


def total_kernel(part, whole, landed, send_one, recv_one, send_two, recv_two):
    own = lax.axis_index("tensor")
    greet(["tensor"])
    one = []
    for distance in range(1, PEERS):
        peer = around("tensor", distance)
        one.append(
            send(part.at[peer], landed.at[distance - 1], send_one, recv_one, distance - 1, "tensor", peer)
        )
    total = part[own].astype(jnp.float32)
    for slot, copy in enumerate(one):
        copy.wait_recv()
        total = total + landed[slot].astype(jnp.float32)
    whole[own] = total.astype(whole.dtype)
    two = []
    for distance in range(1, PEERS):
        peer = around("tensor", distance)
        two.append(
            send(whole.at[own], whole.at[own], send_two, recv_two, distance - 1, "tensor", peer)
        )
    for copy in two:
        copy.wait()
    for copy in one:
        copy.wait_send()


def sum_heads(part):
    if not use_kernels():
        return lax.psum(part, "tensor")
    length, width = part.shape
    split = part.reshape(PEERS, length // PEERS, width)
    return pl.pallas_call(
        total_kernel,
        out_shape=jax.ShapeDtypeStruct(split.shape, split.dtype),
        in_specs=[VMEM],
        out_specs=VMEM,
        scratch_shapes=[pltpu.VMEM((PEERS - 1,) + split.shape[1:], split.dtype)] + sems(3) + sems(3),
        compiler_params=params(2),
    )(split).reshape(length, width)


def joined(parts):
    count, groups, capacity, width = parts.shape
    return jnp.concatenate(
        [parts[index].reshape(groups * capacity, width) for index in range(count)], axis=-1
    )


def share_rows(own_rows, pick, rows, whole, first, second):
    own = lax.axis_index("tensor")
    expert = lax.axis_index("expert")
    rows[...] = (
        lax.dot_general(
            pick[...], own_rows[...], (((0,), (0,)), ((), ())), preferred_element_type=jnp.float32
        )
        .astype(rows.dtype)
        .reshape(rows.shape)
    )
    greet(["tensor", "expert"])
    one = []
    for distance in range(1, PEERS):
        peer = around("expert", distance)
        one.append(send(rows.at[peer], whole.at[own, expert], *first, distance - 1, "expert", peer))
    whole[own, expert] = rows[expert]
    for copy in one:
        copy.wait_recv()
    two = []
    for distance in range(1, PEERS):
        peer = around("tensor", distance)
        two.append(send(whole.at[own], whole.at[own], *second, distance - 1, "tensor", peer))
    for copy in two:
        copy.wait_recv()
    return one + two


def return_rows(values, pick, part, landed, reduced, arrived, back, out, first, second, third, beside):
    own = lax.axis_index("tensor")
    expert = lax.axis_index("expert")
    width = part.shape[3]
    for index in range(PEERS):
        part[index] = (
            values[:, index * width : (index + 1) * width].astype(part.dtype).reshape(part.shape[1:])
        )
    one = []
    for distance in range(1, PEERS):
        peer = around("tensor", distance)
        one.append(send(part.at[peer], landed.at[distance - 1], *first, distance - 1, "tensor", peer))
    if beside is not None:
        beside()
    for copy in one:
        copy.wait_recv()
    total = part[own].astype(jnp.float32)
    for slot in range(PEERS - 1):
        total = total + landed[slot].astype(jnp.float32)
    reduced[...] = total.astype(reduced.dtype)
    two = []
    for distance in range(1, PEERS):
        peer = around("expert", distance)
        two.append(send(reduced.at[peer], arrived.at[expert], *second, distance - 1, "expert", peer))
    arrived[expert] = reduced[expert]
    for copy in two:
        copy.wait_recv()
    groups, capacity, width = arrived.shape
    back[own] = jnp.dot(
        pick[...],
        arrived[...].reshape(groups * capacity, width),
        preferred_element_type=jnp.float32,
    ).astype(back.dtype)
    three = []
    for distance in range(1, PEERS):
        peer = around("tensor", distance)
        three.append(send(back.at[own], back.at[own], *third, distance - 1, "tensor", peer))
    for copy in three:
        copy.wait_recv()
    out[...] = jnp.concatenate([back[index] for index in range(PEERS)], axis=-1)
    return one + two + three


def expert_kernel(
    own_rows, pick, weight_in, weight_out,
    out, groups, hidden_out, active_out,
    rows, landed, part, reduced, arrived, back, whole, *pairs,
):
    pairs = [pairs[2 * index : 2 * index + 2] for index in range(5)]
    copies = share_rows(own_rows, pick, rows, whole, pairs[0], pairs[1])
    together = joined(whole)
    groups[...] = together
    hidden = jnp.dot(together, weight_in[...], preferred_element_type=jnp.float32)
    active = jax.nn.gelu(hidden).astype(jnp.bfloat16)
    values = jnp.dot(active, weight_out[...], preferred_element_type=jnp.float32)

    def keep():
        hidden_out[...] = hidden
        active_out[...] = active

    copies += return_rows(
        values, pick, part, landed, reduced, arrived, back, out, pairs[2], pairs[3], pairs[4], keep
    )
    for copy in copies:
        copy.wait_send()


def gelu_slope(values):
    scale = (2.0 / math.pi) ** 0.5
    square = values * values
    bent = jnp.tanh(scale * values * (1.0 + 0.044715 * square))
    return 0.5 * (1.0 + bent) + 0.5 * values * (1.0 - bent * bent) * scale * (
        1.0 + 3 * 0.044715 * square
    )


def expert_back_kernel(
    own_rows, pick, weight_in, weight_out, groups, hidden, active,
    out, grad_in, grad_out,
    rows, landed, part, reduced, arrived, back, whole, *pairs,
):
    pairs = [pairs[2 * index : 2 * index + 2] for index in range(5)]
    copies = share_rows(own_rows, pick, rows, whole, pairs[0], pairs[1])
    together = joined(whole)
    grad_active = lax.dot_general(
        together, weight_out[...], (((1,), (1,)), ((), ())), preferred_element_type=jnp.float32
    )
    grad_hidden = (grad_active * gelu_slope(hidden[...])).astype(jnp.bfloat16)
    values = lax.dot_general(
        grad_hidden, weight_in[...], (((1,), (1,)), ((), ())), preferred_element_type=jnp.float32
    )

    def weights():
        grad_in[...] = lax.dot_general(
            groups[...], grad_hidden, (((0,), (0,)), ((), ())), preferred_element_type=jnp.float32
        ).astype(grad_in.dtype)
        grad_out[...] = lax.dot_general(
            active[...], together, (((0,), (0,)), ((), ())), preferred_element_type=jnp.float32
        ).astype(grad_out.dtype)

    copies += return_rows(
        values, pick, part, landed, reduced, arrived, back, out, pairs[2], pairs[3], pairs[4], weights
    )
    for copy in copies:
        copy.wait_send()


def expert_call(kernel, number, outs, experts, capacity, operands):
    length, width = operands[0].shape
    low = jnp.bfloat16
    block = (experts, capacity, width)
    return pl.pallas_call(
        kernel,
        out_shape=outs,
        in_specs=[VMEM] * len(operands),
        out_specs=[VMEM] * len(outs),
        scratch_shapes=[
            pltpu.VMEM(block, low),
            pltpu.VMEM((PEERS - 1,) + block, low),
            pltpu.VMEM((PEERS,) + block, low),
            pltpu.VMEM(block, low),
            pltpu.VMEM(block, low),
            pltpu.VMEM((PEERS, length, width), low),
            pltpu.VMEM((PEERS,) + block, low),
        ]
        + sems(3) * 5,
        compiler_params=params(number),
    )(*operands)


def to_experts(own_rows, pick, experts, capacity):
    rows = lax.dot_general(
        pick, own_rows, (((0,), (0,)), ((), ())), preferred_element_type=jnp.float32
    ).astype(jnp.bfloat16)
    arrived = lax.all_to_all(
        rows.reshape(experts, capacity, -1), "expert", split_axis=0, concat_axis=0, tiled=True
    )
    return lax.all_gather(arrived.reshape(experts * capacity, -1), "tensor", axis=1, tiled=True)


def from_experts(values, pick, experts, capacity):
    share = lax.psum_scatter(
        values.astype(jnp.bfloat16), "tensor", scatter_dimension=1, tiled=True
    )
    returned = lax.all_to_all(
        share.reshape(experts, capacity, -1), "expert", split_axis=0, concat_axis=0, tiled=True
    )
    picked = jnp.dot(
        pick, returned.reshape(experts * capacity, -1), preferred_element_type=jnp.float32
    ).astype(jnp.bfloat16)
    return lax.all_gather(picked, "tensor", axis=1, tiled=True)


def run_experts(own_rows, pick, weight_in, weight_out, experts, capacity):
    if use_kernels():
        length = own_rows.shape[0]
        width, hidden_width = weight_in.shape
        slots = experts * capacity
        return expert_call(
            expert_kernel,
            3,
            [
                jax.ShapeDtypeStruct((length, width), jnp.bfloat16),
                jax.ShapeDtypeStruct((slots, width), jnp.bfloat16),
                jax.ShapeDtypeStruct((slots, hidden_width), jnp.float32),
                jax.ShapeDtypeStruct((slots, hidden_width), jnp.bfloat16),
            ],
            experts,
            capacity,
            (own_rows, pick, weight_in, weight_out),
        )
    groups = to_experts(own_rows, pick, experts, capacity)
    hidden = jnp.dot(groups, weight_in, preferred_element_type=jnp.float32)
    active = jax.nn.gelu(hidden).astype(jnp.bfloat16)
    values = jnp.dot(active, weight_out, preferred_element_type=jnp.float32)
    return (from_experts(values, pick, experts, capacity), groups, hidden, active)


def run_experts_back(
    own_rows, pick, weight_in, weight_out, groups, hidden, active, experts, capacity
):
    if use_kernels():
        return expert_call(
            expert_back_kernel,
            4,
            [
                jax.ShapeDtypeStruct((own_rows.shape[0], weight_in.shape[0]), jnp.bfloat16),
                jax.ShapeDtypeStruct(weight_in.shape, jnp.bfloat16),
                jax.ShapeDtypeStruct(weight_out.shape, jnp.bfloat16),
            ],
            experts,
            capacity,
            (own_rows, pick, weight_in, weight_out, groups, hidden, active),
        )
    grad_groups = to_experts(own_rows, pick, experts, capacity)
    grad_active = lax.dot_general(
        grad_groups, weight_out, (((1,), (1,)), ((), ())), preferred_element_type=jnp.float32
    )
    grad_hidden = (grad_active * gelu_slope(hidden)).astype(jnp.bfloat16)
    values = lax.dot_general(
        grad_hidden, weight_in, (((1,), (1,)), ((), ())), preferred_element_type=jnp.float32
    )
    grad_in = lax.dot_general(
        groups, grad_hidden, (((0,), (0,)), ((), ())), preferred_element_type=jnp.float32
    ).astype(jnp.bfloat16)
    grad_out = lax.dot_general(
        active, grad_groups, (((0,), (0,)), ((), ())), preferred_element_type=jnp.float32
    ).astype(jnp.bfloat16)
    return (from_experts(values, pick, experts, capacity), grad_in, grad_out)


def finish_kernel(
    normed, joint, attn, mixed, small, give_in, give_out,
    grads_out, small_out, came_in, came_out,
    give, give_small, came, came_small, summed, summed_small, landed, landed_small,
    near_send, near_recv, far_send, far_recv,
):
    section = lax.axis_index("section")
    expert = lax.axis_index("expert")
    other = 1 - section

    def product(layer):
        dims = (((0,), (0,)), ((), ()))
        left = lax.dot_general(
            normed[layer], joint[layer], dims, preferred_element_type=jnp.float32
        )
        right = lax.dot_general(
            attn[layer], mixed[layer], dims, preferred_element_type=jnp.float32
        )
        return jnp.concatenate([left, right], axis=-1).reshape(summed.shape)

    give[...] = product(other).astype(give.dtype)
    give_small[...] = small[other].astype(give_small.dtype)
    greet(["expert"], sibling=True)
    near = []
    for distance in range(PEERS):
        peer = around("expert", distance)
        near.append(
            send(give.at[peer], came.at[peer], near_send, near_recv, distance, "section", other)
        )
    near.append(send(give_small, came_small, near_send, near_recv, 4, "section", other))
    near.append(send(give_in, came_in, near_send, near_recv, 5, "section", other))
    near.append(send(give_out, came_out, near_send, near_recv, 6, "section", other))
    summed[...] = product(section).astype(summed.dtype)
    copies = []
    for distance in (1, 2, 3, 0):
        peer = around("expert", distance)
        near[distance].wait_recv()
        summed[peer] = (
            summed[peer].astype(jnp.float32) + came[peer].astype(jnp.float32)
        ).astype(summed.dtype)
        if distance:
            slot = distance - 1
            copies.append(
                send(summed.at[peer], landed.at[slot], far_send, far_recv, slot, "expert", peer)
            )
    near[4].wait_recv()
    summed_small[...] = (small[section] + came_small[...].astype(jnp.float32)).astype(
        summed_small.dtype
    )
    for distance in range(1, PEERS):
        peer = around("expert", distance)
        slot = distance - 1
        copies.append(
            send(
                summed_small.at[peer], landed_small.at[slot], far_send, far_recv, 3 + slot, "expert", peer
            )
        )
    grads_out[...] = summed[expert].astype(jnp.float32)
    small_out[...] = summed_small[expert].astype(jnp.float32)
    for slot in range(PEERS - 1):
        copies[slot].wait_recv()
        grads_out[...] += landed[slot].astype(jnp.float32)
        copies[3 + slot].wait_recv()
        small_out[...] += landed_small[slot].astype(jnp.float32)
    near[5].wait_recv()
    near[6].wait_recv()
    for copy in near + copies:
        copy.wait_send()


def reduce_grads(normed, joint, attn, mixed, small, give_in, give_out):
    experts = lax.axis_size("expert")
    layers, length, width = normed.shape
    piece = width // experts
    columns = joint.shape[2] + mixed.shape[2]
    low = jnp.bfloat16
    if not use_kernels():
        section = lax.axis_index("section")
        outer = lambda a, b: jnp.einsum(
            "lta,ltb->lab", a, b, preferred_element_type=jnp.float32
        )
        grads = jnp.concatenate([outer(normed, joint), outer(attn, mixed)], axis=2).reshape(
            layers, experts, piece, columns
        )
        results = []
        for part in (grads, small):
            scattered = lax.psum_scatter(
                part.astype(low), "expert", scatter_dimension=1, tiled=False
            ).astype(jnp.float32)
            own = lax.dynamic_index_in_dim(scattered, section, 0, keepdims=False)
            far = lax.dynamic_index_in_dim(scattered, 1 - section, 0, keepdims=False).astype(low)
            came = lax.ppermute(far, "section", [(0, 1), (1, 0)])
            results.append(own + came.astype(jnp.float32))
        swap = lambda a: lax.ppermute(a, "section", [(0, 1), (1, 0)])
        return results + [swap(give_in), swap(give_out)]
    wide = (PEERS, piece, columns)
    slim = (PEERS, piece, 128)
    return pl.pallas_call(
        finish_kernel,
        out_shape=[
            jax.ShapeDtypeStruct((piece, columns), jnp.float32),
            jax.ShapeDtypeStruct((piece, 128), jnp.float32),
            jax.ShapeDtypeStruct(give_in.shape, low),
            jax.ShapeDtypeStruct(give_out.shape, low),
        ],
        in_specs=[VMEM] * 7,
        out_specs=[VMEM] * 4,
        scratch_shapes=[pltpu.VMEM(shape, low) for _ in range(3) for shape in (wide, slim)]
        + [
            pltpu.VMEM((PEERS - 1, piece, columns), low),
            pltpu.VMEM((PEERS - 1, piece, 128), low),
        ]
        + sems(7)
        + sems(6),
        compiler_params=params(5),
    )(normed, joint, attn, mixed, small, give_in, give_out)


def own_features(rows):
    width = rows.shape[1] // lax.axis_size("tensor")
    return lax.dynamic_slice_in_dim(rows, lax.axis_index("tensor") * width, width, 1)


def slots_for(length, experts):
    capacity = 5 * length // (4 * experts)
    return -(-capacity // 16) * 16


def offset_buckets(length):
    half_count = BUCKETS // 2
    exact_count = half_count // 2
    offsets = jnp.arange(2 * length, dtype=jnp.int32) - (length - 1)
    distance = jnp.abs(offsets)
    larger = jnp.full_like(distance, exact_count)
    for level_index in range(1, half_count - exact_count):
        border = int(
            math.ceil(
                exact_count * (128.0 / exact_count) ** (level_index / (half_count - exact_count))
                - 1e-09
            )
        )
        larger = larger + (distance >= border).astype(jnp.int32)
    bucket = jnp.where(distance < exact_count, distance, larger)
    return bucket + jnp.where(offsets > 0, half_count, 0)


def spread_offsets(per_offset, length):
    heads_here = per_offset.shape[0]
    tiled = jnp.tile(per_offset, (1, length))[:, : length * (2 * length - 1)]
    skewed = tiled.reshape(heads_here, length, 2 * length - 1)
    return skewed[:, :, length - 1 :]


def collect_offsets(grid_values, length):
    heads_here = grid_values.shape[0]
    padded = jnp.pad(grid_values, ((0, 0), (0, 0), (length - 1, 0)))
    flat = jnp.pad(padded.reshape(heads_here, length * (2 * length - 1)), ((0, 0), (0, length)))
    return jnp.sum(flat.reshape(heads_here, length, 2 * length), axis=1, dtype=jnp.float32)


def rms_scale(values, gain_vector):
    return (
        values * lax.rsqrt(jnp.mean(values * values, axis=-1, keepdims=True) + 1e-06) * gain_vector
    )


def slot_places(route_ids, experts, capacity):
    chosen = route_ids[:, None] == jnp.arange(experts, dtype=jnp.int32)[None, :]
    counts = jnp.cumsum(chosen.astype(jnp.int32), axis=0)
    slot_number = jnp.sum(jnp.where(chosen, counts, 0), axis=-1) - 1
    return (chosen, route_ids * capacity + slot_number)


def position_bias(offset_table, bias_table, length):
    per_offset = jnp.dot(
        offset_table, bias_table.astype(jnp.float32), precision=lax.Precision.HIGHEST
    )
    return spread_offsets(per_offset.T, length)


def attention_probs(query_heads, key_heads, rel_bias, labels, head_size):
    scores = (
        jnp.einsum("qhe,khe->hqk", query_heads, key_heads, preferred_element_type=jnp.float32)
        * head_size ** (-0.5)
        + rel_bias
    )
    same_doc = labels[:, None] == labels[None, :]
    return jnp.where(same_doc[None], scores, -1000000000.0)


def forward_layer(layer_in, weights, route_ids, labels, offset_table, weight_in, weight_out):
    gain_one, joint_weight, attn_out_weight, bias_table, gain_two, router_matrix = weights
    length, model_width = layer_in.shape
    heads_here = bias_table.shape[1]
    head_size = attn_out_weight.shape[1] // heads_here
    experts = router_matrix.shape[1]
    capacity = slots_for(length, experts)
    input_float = layer_in.astype(jnp.float32)
    normed = rms_scale(input_float, gain_one).astype(jnp.bfloat16)
    joint_heads = jnp.dot(normed, joint_weight, preferred_element_type=jnp.float32).astype(
        jnp.bfloat16
    )
    query_heads, key_heads, value_heads = [
        part.reshape(length, heads_here, head_size) for part in jnp.split(joint_heads, 3, axis=1)
    ]
    rel_bias = position_bias(offset_table, bias_table, length)
    scores = attention_probs(query_heads, key_heads, rel_bias, labels, head_size)
    log_total = jax.nn.logsumexp(scores, axis=-1)
    probs_low = jnp.exp(scores - log_total[..., None]).astype(jnp.bfloat16)
    mixed_heads = (
        jnp.einsum("hqk,khe->qhe", probs_low, value_heads, preferred_element_type=jnp.float32)
        .astype(jnp.bfloat16)
        .reshape(length, heads_here * head_size)
    )
    partial_out = lax.dot_general(
        mixed_heads, attn_out_weight, (((1,), (1,)), ((), ())), preferred_element_type=jnp.float32
    )
    residual = input_float + sum_heads(partial_out.astype(jnp.bfloat16)).astype(jnp.float32)
    normed_two = rms_scale(residual, gain_two)
    logits = jnp.dot(normed_two, router_matrix, precision=lax.Precision.HIGHEST)
    router_probs = jax.nn.softmax(logits, axis=-1)
    chosen, slot_index = slot_places(route_ids, experts, capacity)
    gate_value = jnp.sum(jnp.where(chosen, router_probs, 0.0), axis=-1, keepdims=True)
    pick = (
        slot_index[:, None] == jnp.arange(experts * capacity, dtype=jnp.int32)[None, :]
    ).astype(jnp.bfloat16)
    expert_low, groups, hidden, active = run_experts(
        own_features(normed_two).astype(jnp.bfloat16),
        pick,
        weight_in,
        weight_out,
        experts,
        capacity,
    )
    output = (residual + gate_value * expert_low.astype(jnp.float32)).astype(jnp.bfloat16)
    kept_state = (
        layer_in,
        normed,
        query_heads,
        key_heads,
        value_heads,
        mixed_heads,
        log_total,
        residual,
        router_probs,
        gate_value,
        pick,
        groups,
        hidden,
        active,
        expert_low,
    )
    return (output, kept_state)


def backward_layer(
    grad_out, kept_state, weights, route_ids, labels, offset_table, weight_in, weight_out
):
    (
        layer_in,
        normed,
        query_heads,
        key_heads,
        value_heads,
        mixed_heads,
        log_total,
        residual,
        router_probs,
        gate_value,
        pick,
        groups,
        hidden,
        active,
        expert_low,
    ) = kept_state
    gain_one, joint_weight, attn_out_weight, bias_table, gain_two, router_matrix = weights
    length, model_width = layer_in.shape
    heads_here = bias_table.shape[1]
    head_size = attn_out_weight.shape[1] // heads_here
    experts = router_matrix.shape[1]
    capacity = slots_for(length, experts)
    grad_float = grad_out.astype(jnp.float32)
    grad_gate = jnp.sum(grad_float * expert_low.astype(jnp.float32), axis=-1, keepdims=True)
    grad_value = (gate_value * grad_float).astype(jnp.bfloat16)
    grad_rows, grad_weight_in, grad_weight_out = run_experts_back(
        own_features(grad_value),
        pick,
        weight_in,
        weight_out,
        groups,
        hidden,
        active,
        experts,
        capacity,
    )
    grad_normed_two = grad_rows.astype(jnp.float32)
    chosen = route_ids[:, None] == jnp.arange(experts, dtype=jnp.int32)[None, :]
    grad_logits = grad_gate * gate_value * (chosen.astype(jnp.float32) - router_probs)
    grad_normed_two = grad_normed_two + lax.dot_general(
        grad_logits, router_matrix, (((1,), (1,)), ((), ())), precision=lax.Precision.HIGHEST
    )
    normed_two, norm_pull = jax.vjp(rms_scale, residual, gain_two)
    grad_router = lax.dot_general(
        normed_two, grad_logits, (((0,), (0,)), ((), ())), precision=lax.Precision.HIGHEST
    )
    grad_residual, grad_gain_two = norm_pull(grad_normed_two)
    grad_residual = grad_residual + grad_float
    grad_attn = grad_residual.astype(jnp.bfloat16)
    grad_mixed = (
        jnp.dot(grad_attn, attn_out_weight, preferred_element_type=jnp.float32)
        .astype(jnp.bfloat16)
        .reshape(length, heads_here, head_size)
    )
    rel_bias = position_bias(offset_table, bias_table, length)
    scores = attention_probs(query_heads, key_heads, rel_bias, labels, head_size)
    probs_float = jnp.exp(scores - log_total[..., None])
    probs_low = probs_float.astype(jnp.bfloat16)
    grad_probs = jnp.einsum(
        "qhe,khe->hqk", grad_mixed, value_heads, preferred_element_type=jnp.float32
    )
    grad_scores = (
        probs_float * (grad_probs - jnp.sum(probs_float * grad_probs, axis=-1, keepdims=True))
    ).astype(jnp.bfloat16)
    grad_query = (
        jnp.einsum("hqk,khe->qhe", grad_scores, key_heads, preferred_element_type=jnp.float32)
        * head_size ** (-0.5)
    ).astype(jnp.bfloat16)
    grad_keys = (
        jnp.einsum("hqk,qhe->khe", grad_scores, query_heads, preferred_element_type=jnp.float32)
        * head_size ** (-0.5)
    ).astype(jnp.bfloat16)
    grad_values = jnp.einsum(
        "hqk,qhe->khe", probs_low, grad_mixed, preferred_element_type=jnp.float32
    ).astype(jnp.bfloat16)
    offset_sums = collect_offsets(grad_scores, length)
    grad_table = jnp.einsum("kb,hk->bh", offset_table, offset_sums, precision=lax.Precision.HIGHEST)
    grad_joint = jnp.concatenate(
        [
            part.reshape(length, heads_here * head_size)
            for part in (grad_query, grad_keys, grad_values)
        ],
        axis=1,
    )
    grad_normed_part = lax.dot_general(
        grad_joint, joint_weight, (((1,), (1,)), ((), ())), preferred_element_type=jnp.float32
    )
    grad_normed = sum_heads(grad_normed_part.astype(jnp.bfloat16)).astype(jnp.float32)
    input_pull = jax.vjp(rms_scale, layer_in.astype(jnp.float32), gain_one)[1]
    grad_input_part, grad_gain_one = input_pull(grad_normed)
    grad_input = (grad_residual + grad_input_part).astype(jnp.bfloat16)
    small_terms = (grad_gain_one, grad_table, grad_gain_two, grad_router)
    return (
        grad_input,
        small_terms,
        (normed, grad_joint, grad_attn, mixed_heads),
        (grad_weight_in, grad_weight_out),
    )


def pack_terms(small_terms, expert_count):
    gain_one, table, gain_two, router = small_terms
    width = gain_one.shape[0]
    piece = width // expert_count
    rows = table.shape[0] // expert_count
    table = jnp.pad(
        table.reshape(expert_count, rows, -1), ((0, 0), (0, piece - rows), (0, 0))
    ).reshape(width, -1)
    used = 2 + table.shape[1] + router.shape[1]
    return jnp.concatenate(
        [
            gain_one[:, None],
            gain_two[:, None],
            table,
            router,
            jnp.zeros((width, 128 - used), jnp.float32),
        ],
        axis=1,
    ).reshape(expert_count, piece, 128)


def swap_micro(per_layer):
    section = lax.axis_index("section")
    own = jnp.where(section == 0, per_layer[0], per_layer[1])
    other = jnp.where(section == 0, per_layer[1], per_layer[0])
    came = lax.ppermute(other, "section", [(0, 1), (1, 0)])
    return jnp.where(
        section == 0, jnp.stack([own, came]), jnp.stack([came, own])
    )[None]


def local(
    inputs,
    cotangent,
    attn_gain,
    query_weight,
    key_weight,
    value_weight,
    out_weight,
    rel_table,
    ffn_gain,
    router_weight,
    expert_in,
    expert_out,
    routes,
    segments,
):
    section = lax.axis_index("section")
    layers = lax.axis_size("section")
    expert_count = lax.axis_size("expert")
    micro_count, length, model_width = inputs.shape
    heads_here = rel_table.shape[2]
    experts = router_weight.shape[2]
    piece = attn_gain.shape[1]
    attn = jnp.concatenate(
        [query_weight[0], key_weight[0], value_weight[0], out_weight[0]], axis=1
    )
    joint_columns = 3 * query_weight.shape[2]
    used = 2 + heads_here + experts
    small = jnp.concatenate(
        [
            attn_gain[0][:, None],
            ffn_gain[0][:, None],
            jnp.pad(rel_table[0], ((0, piece - rel_table.shape[1]), (0, 0))),
            router_weight[0],
            jnp.zeros((piece, 128 - used), jnp.bfloat16),
        ],
        axis=1,
    )
    ids = jnp.pad(routes[0, :, :, 0].astype(jnp.bfloat16), ((0, 16 - micro_count), (0, 0)))
    attn_all, small_all, ids_all, in_all, out_all = collect_weights(
        attn, small, ids, expert_in[0, 0], expert_out[0, 0]
    )
    offset_ids = offset_buckets(length)
    offset_table = (offset_ids[:, None] == jnp.arange(BUCKETS, dtype=jnp.int32)[None, :]).astype(
        jnp.float32
    )
    labels = lax.dynamic_index_in_dim(segments, section, 0, keepdims=False)
    current = lax.dynamic_index_in_dim(inputs, section, 0, keepdims=False)
    layer_weights = []
    kept_list = []
    outputs = []
    for layer in range(layers):
        matrices = attn_all[layer].reshape(model_width, -1)
        columns = small_all[layer]
        flat = columns.reshape(model_width, -1)
        weights = (
            flat[:, 0].astype(jnp.float32),
            matrices[:, :joint_columns],
            matrices[:, joint_columns:],
            columns[:, : rel_table.shape[1], 2 : 2 + heads_here].reshape(BUCKETS, heads_here),
            flat[:, 1].astype(jnp.float32),
            flat[:, 2 + heads_here : used].astype(jnp.float32),
        )
        route_ids = lax.dynamic_index_in_dim(ids_all[layer], section, 0, keepdims=False).astype(
            jnp.int32
        )
        layer_weights.append((weights, route_ids))
        current, kept_state = forward_layer(
            current, weights, route_ids, labels, offset_table, in_all[layer], out_all[layer]
        )
        kept_list.append(kept_state)
        outputs.append(current)
    grad = lax.dynamic_index_in_dim(cotangent, section, 0, keepdims=False)
    input_grads = [None] * layers
    packs = [None] * layers
    expert_packs = [None] * layers
    for layer in reversed(range(layers)):
        weights, route_ids = layer_weights[layer]
        grad, small_terms, wide_terms, expert_terms = backward_layer(
            grad,
            kept_list[layer],
            weights,
            route_ids,
            labels,
            offset_table,
            in_all[layer],
            out_all[layer],
        )
        input_grads[layer] = grad
        packs[layer] = wide_terms + (pack_terms(small_terms, expert_count),)
        expert_packs[layer] = expert_terms
    given = [
        jnp.where(section == 0, expert_packs[1][index], expert_packs[0][index])
        for index in range(2)
    ]
    kept = [
        jnp.where(section == 0, expert_packs[0][index], expert_packs[1][index])
        for index in range(2)
    ]
    grads, small_grads, *came = reduce_grads(*[jnp.stack(pair) for pair in zip(*packs)], *given)
    grad_in, grad_out = [
        kept[index].astype(jnp.float32) + came[index].astype(jnp.float32) for index in range(2)
    ]
    parts = jnp.split(grads, 4, axis=1)
    return (
        swap_micro(outputs),
        swap_micro(input_grads),
        small_grads[None, :, 0],
        parts[0][None],
        parts[1][None],
        parts[2][None],
        parts[3][None],
        small_grads[None, : rel_table.shape[1], 2 : 2 + heads_here],
        small_grads[None, :, 1],
        small_grads[None, :, 2 + heads_here : used],
        grad_in[None, None],
        grad_out[None, None],
    )


def solution(mesh):
    return jax.shard_map(
        local,
        mesh=mesh,
        in_specs=(
            P(None, "expert", None),
            P(None, "expert", None),
            P("section", "expert"),
            P("section", "expert", "tensor"),
            P("section", "expert", "tensor"),
            P("section", "expert", "tensor"),
            P("section", "expert", "tensor"),
            P("section", "expert", "tensor"),
            P("section", "expert"),
            P("section", "expert", None),
            P("section", "expert", None, "tensor"),
            P("section", "expert", "tensor", None),
            P("section", None, "expert", None),
            P(None, "expert"),
        ),
        out_specs=(
            P("section", None, "expert", None),
            P("section", None, "expert", None),
            P("section", "expert"),
            P("section", "expert", "tensor"),
            P("section", "expert", "tensor"),
            P("section", "expert", "tensor"),
            P("section", "expert", "tensor"),
            P("section", "expert", "tensor"),
            P("section", "expert"),
            P("section", "expert", None),
            P("section", "expert", None, "tensor"),
            P("section", "expert", "tensor", None),
        ),
        check_vma=False,
    )
```
